512 devices in a mesh: section: 32 (over z, core), tensor: 16 (over x, y).
Axes of the slice: x: 4, y: 4, z: 16, core: 2. Of those that a mesh axis runs over, the one named last changes fastest.
Arguments:
- patches: bfloat16 [64, 128, 3200], P('section', 'tensor')
- plan: int32 [64], replicated, may hold values from 0 to 63, as said below
- norm_gain: float32 [3200], replicated, may hold values from 0.5 to 2
- proj_in: bfloat16 [3200, 6400], P('section', 'tensor'), may hold values from -0.109375 to 0.109375
- proj_out: bfloat16 [6400, 3200], P('tensor', 'section'), may hold values from -0.078125 to 0.078125
- layer_scale: float32 [3200], replicated, may hold values from 0.3 to 1.5
Outputs:
- delivered: bfloat16 [64, 128, 3200], P('section', 'tensor')
The draws below stay inside these ranges and needn't reach their ends.
Inputs may be any that keep to these rules, and one draw needn't show every extreme that they name: `plan`: a permutation of the 64 block numbers; position p lies on section p // 2, block b starts on section b // 2; the 2 blocks that start on one section go to 2 different sections.
All inputs are finite; a program needn't handle non-finite values.
Results may differ from the reference program's by a relative error of at most 0.009.
Values may be sent and summed in bfloat16 or wider, within the bound.
No kernel may reach another device: no remote copies, remote signals or barrier semaphores. Data moves between devices by JAX's collectives and lax.ppermute only.
A program may use at most 64 MiB of HBM per device.

```python
import math
import jax
import jax.numpy as jnp
from jax import lax

E = 3200
F = 6400
BLOCK = 128
BLK_DEV = 2
NBLK = 64
N_TENSOR = 16


def draw_patches(key, part):
    key = jax.random.fold_in(key, 11)
    key_base, key_rows, key_cols = jax.random.split(key, 3)
    row_scale = jnp.exp(jax.random.uniform(key_rows, (NBLK, BLOCK, 1), minval=math.log(0.3), maxval=math.log(3.0)))
    col_scale = jnp.exp(jax.random.uniform(key_cols, (1, 1, E), minval=math.log(0.5), maxval=math.log(2.0)))
    values = jax.random.normal(key_base, (NBLK, BLOCK, E))
    return (values * row_scale * col_scale).astype(jnp.bfloat16)


def draw_plan(key, part):
    key = jax.random.fold_in(key, 23)
    key_perm, key_shift, key_slot = jax.random.split(key, 3)
    sections = NBLK // BLK_DEV
    section_perm = jax.random.permutation(key_perm, sections)
    inverse = jnp.argsort(section_perm)
    shifts = jnp.concatenate([jnp.zeros((1,), jnp.int32), (jax.random.permutation(key_shift, sections - 1)[:BLK_DEV - 1] + 1).astype(jnp.int32)])
    target = jnp.arange(sections, dtype=jnp.int32)[:, None]
    slot_ids = jnp.arange(BLK_DEV, dtype=jnp.int32)[None, :]
    source = (inverse[target].astype(jnp.int32) - shifts[slot_ids]) % sections
    blocks = source * BLK_DEV + slot_ids
    scores = jax.random.randint(key_slot, (sections, BLK_DEV), 0, 1000) * BLK_DEV + slot_ids
    ordering = jnp.argsort(scores, axis=1, stable=True)
    blocks = jnp.take_along_axis(blocks, ordering, axis=1)
    return blocks.reshape(-1).astype(jnp.int32)


def block_levels(own_key, extent, pieces, low, top_value):
    loudness = 1.0
    for position, blocks in pieces:
        draws = jax.random.uniform(jax.random.fold_in(jax.random.fold_in(own_key, 6), position), (blocks,), jnp.float32, low / len(pieces), top_value / len(pieces))
        loudness = loudness * jnp.repeat(jnp.exp(draws), extent[position] // blocks).reshape((-1,) + (1,) * (len(extent) - 1 - position))
    return loudness


def gaussian(stream_key, shape, spread, bound, shards=(), kind=jnp.bfloat16):
    level = block_levels(stream_key, shape, shards, -0.22, 0.18) if shards else 1.0
    entries = jax.random.normal(stream_key, shape, jnp.float32) * spread * level
    return jnp.minimum(jnp.maximum(entries, -bound), bound).astype(kind)


def setup_inputs(seed: int = 0) -> dict:
    key_list = jax.random.split(jax.random.key(seed), 7)
    patches = draw_patches(jax.random.fold_in(key_list[6], 71), 0)
    plan = draw_plan(jax.random.fold_in(key_list[6], 71), 0)
    norm_gain = jnp.clip(jnp.exp(jax.random.uniform(key_list[2], (E,), jnp.float32, math.log(0.5), math.log(2.0))), 0.5, 2.0)
    proj_in = gaussian(key_list[3], (E, F), E ** -0.5, 0.109375, ((0, 32), (1, 16)))
    proj_out = gaussian(key_list[4], (F, E), F ** -0.5, 0.078125, ((0, 16), (1, 32)))
    layer_scale = jnp.clip(jax.random.uniform(key_list[5], (E,), jnp.float32, 0.3, 1.5), 0.3, 1.5)
    return dict(patches=patches, plan=plan, norm_gain=norm_gain, proj_in=proj_in, proj_out=proj_out, layer_scale=layer_scale)


def encode(patch_block, norm_gain, proj_in, proj_out, layer_scale):
    values = patch_block.astype(jnp.float32)
    mean_square = lax.optimization_barrier(jnp.mean(values * values, axis=-1, keepdims=True))
    normed = (values * lax.rsqrt(mean_square + 1e-06) * norm_gain).astype(jnp.bfloat16)
    hidden = jax.nn.gelu(jnp.dot(normed, proj_in, preferred_element_type=jnp.float32), approximate=False).astype(jnp.bfloat16)
    group_size = F // N_TENSOR
    grouped = hidden.reshape(hidden.shape[0], N_TENSOR, group_size).astype(jnp.float32)
    weights = proj_out.reshape(N_TENSOR, group_size, proj_out.shape[1]).astype(jnp.float32)
    products = jnp.einsum('rng,nge->nre', grouped, weights)
    rounded = lax.optimization_barrier(products.astype(jnp.bfloat16)).astype(jnp.float32)
    branch = lax.optimization_barrier(jnp.sum(rounded, axis=0))
    return (values + layer_scale * branch).astype(jnp.bfloat16)

def reference(patches, plan, norm_gain, proj_in, proj_out, layer_scale):
    encoded = lax.map(lambda patch_block: encode(patch_block, norm_gain, proj_in, proj_out, layer_scale), patches)
    return encoded[plan]
```

```python
import functools

import jax
import jax.numpy as jnp
from jax import lax
from jax.experimental import pallas as pl
from jax.experimental.pallas import tpu as pltpu
from jax.sharding import PartitionSpec as P

LANE = 128
VMEM = pl.BlockSpec(memory_space=pltpu.VMEM)
SMEM = pl.BlockSpec(memory_space=pltpu.SMEM)


def call(body, out_shape, in_specs, flops=0, moved=0, n_out=1, scratch=()):
    return pl.pallas_call(
        body,
        out_shape=out_shape,
        in_specs=in_specs,
        out_specs=VMEM if n_out == 1 else [VMEM] * n_out,
        scratch_shapes=list(scratch),
        compiler_params=pltpu.CompilerParams(vmem_limit_bytes=40 * 1024 * 1024),
        cost_estimate=pl.CostEstimate(flops=flops, bytes_accessed=moved, transcendentals=0),
    )


def split_body(x_ref, o_ref):
    blocks, rows, width = x_ref.shape
    for m in range(o_ref.shape[0] // blocks):
        if (m + 1) * LANE <= width:
            for b in range(blocks):
                o_ref[m * blocks + b] = x_ref[b, :, m * LANE : (m + 1) * LANE]
        else:
            for b in range(blocks):
                o_ref[m * blocks + b] = jnp.zeros((rows, LANE), o_ref.dtype)


def order_body(plan_ref, x_ref, o_ref):
    for p in range(o_ref.shape[0]):
        o_ref[p] = x_ref[plan_ref[p]]


def norm_body(x_ref, gain_ref, rows_ref, copies_ref):
    blocks, rows, width = rows_ref.shape
    tiles = width // LANE
    for b in range(blocks):
        whole = jnp.concatenate([x_ref[m * blocks + b] for m in range(tiles)], axis=-1)
        rows_ref[b] = whole
        values = whole.astype(jnp.float32)
        mean_square = jnp.sum(values * values, axis=-1, keepdims=True) * (1.0 / width)
        normed = values * lax.rsqrt(mean_square + 1e-06) * gain_ref[...]
        normed = normed.astype(jnp.bfloat16)
        for t in range(copies_ref.shape[0]):
            copies_ref[t, b] = normed


def mlp_body(x_ref, w_ref, o_ref):
    sections, both, part = w_ref.shape
    hidden_units = both // 2
    total = jnp.zeros((x_ref.shape[0], hidden_units), jnp.float32)
    for s in range(sections):
        total += lax.dot_general(
            x_ref[:, s * part : (s + 1) * part],
            w_ref[s, :hidden_units, :],
            (((1,), (1,)), ((), ())),
            preferred_element_type=jnp.float32,
        )
    hidden = 0.5 * total * (1.0 + lax.erf(total * (0.5**0.5)))
    hidden = hidden.astype(jnp.bfloat16)
    for s in range(sections):
        o_ref[:, s * part : (s + 1) * part] = jnp.dot(
            hidden, w_ref[s, hidden_units:, :], preferred_element_type=jnp.float32
        ).astype(jnp.bfloat16)


def sum_body(x_ref, rows_ref, scale_ref, o_ref):
    blocks = rows_ref.shape[0]
    for b in range(blocks):
        branch = x_ref[0, b].astype(jnp.float32)
        for t in range(1, x_ref.shape[0]):
            branch += x_ref[t, b].astype(jnp.float32)
        values = rows_ref[b].astype(jnp.float32)
        o_ref[b] = (values + scale_ref[...] * branch).astype(o_ref.dtype)


def local(sections, groups, patches, plan, norm_gain, proj_in, proj_out, layer_scale):
    blocks, rows, width = patches.shape
    bf16 = jnp.bfloat16
    weights = jnp.concatenate([proj_in.T, proj_out], axis=0)
    weights = lax.all_gather(weights, "section", axis=0, tiled=False)

    shape = jax.ShapeDtypeStruct((sections * blocks, rows, LANE), bf16)
    tiles = call(split_body, shape, [VMEM])(patches)
    tiles = lax.all_to_all(tiles, "section", 0, 0, tiled=True)
    tiles = call(order_body, shape, [SMEM, VMEM])(plan, tiles)
    tiles = lax.all_to_all(tiles, "section", 0, 0, tiled=True)
    own, copies = call(
        norm_body,
        (
            jax.ShapeDtypeStruct((blocks, rows, width), bf16),
            jax.ShapeDtypeStruct((groups, blocks, rows, width), bf16),
        ),
        [VMEM, VMEM],
        n_out=2,
    )(tiles, norm_gain.reshape(1, width))

    all_rows = groups * blocks * rows
    normed = lax.all_to_all(copies, "tensor", 0, 0, tiled=True)
    partial_sum = call(
        mlp_body,
        jax.ShapeDtypeStruct((all_rows, width), bf16),
        [VMEM, VMEM],
        flops=4 * all_rows * width * proj_in.shape[1],
        moved=10 * 1024 * 1024,
    )(normed.reshape(all_rows, width), weights)
    terms = lax.all_to_all(
        partial_sum.reshape(groups, blocks, rows, width), "tensor", 0, 0, tiled=True
    )
    return call(
        sum_body, jax.ShapeDtypeStruct((blocks, rows, width), bf16), [VMEM, VMEM, VMEM]
    )(terms, own, layer_scale.reshape(1, width))


def solution(mesh):
    return jax.shard_map(
        functools.partial(local, mesh.shape["section"], mesh.shape["tensor"]),
        mesh=mesh,
        in_specs=(
            P("section", "tensor", None),
            P(),
            P(),
            P("section", "tensor"),
            P("tensor", "section"),
            P(),
        ),
        out_specs=P("section", "tensor", None),
        check_vma=False,
    )
```

```python
import functools

import jax
import jax.numpy as jnp
from jax import lax
from jax.experimental import pallas as pl
from jax.experimental.pallas import tpu as pltpu
from jax.sharding import PartitionSpec as P

LANE = 128
VMEM = pl.BlockSpec(memory_space=pltpu.VMEM)
SMEM = pl.BlockSpec(memory_space=pltpu.SMEM)


def call(body, out_shape, in_specs, flops=0, moved=0, n_out=1, scratch=()):
    return pl.pallas_call(
        body,
        out_shape=out_shape,
        in_specs=in_specs,
        out_specs=VMEM if n_out == 1 else [VMEM] * n_out,
        scratch_shapes=list(scratch),
        compiler_params=pltpu.CompilerParams(vmem_limit_bytes=40 * 1024 * 1024),
        cost_estimate=pl.CostEstimate(flops=flops, bytes_accessed=moved, transcendentals=0),
    )


def split_body(x_ref, o_ref):
    blocks, rows, width = x_ref.shape
    for m in range(o_ref.shape[0] // blocks):
        if (m + 1) * LANE <= width:
            for b in range(blocks):
                o_ref[m * blocks + b] = x_ref[b, :, m * LANE : (m + 1) * LANE]
        else:
            for b in range(blocks):
                o_ref[m * blocks + b] = jnp.zeros((rows, LANE), o_ref.dtype)


def order_body(plan_ref, x_ref, o_ref):
    for p in range(o_ref.shape[0]):
        o_ref[p] = x_ref[plan_ref[p]]


def norm_body(x_ref, gain_ref, rows_ref, copies_ref):
    blocks, rows, width = rows_ref.shape
    tiles = width // LANE
    for b in range(blocks):
        whole = jnp.concatenate([x_ref[m * blocks + b] for m in range(tiles)], axis=-1)
        rows_ref[b] = whole
        values = whole.astype(jnp.float32)
        mean_square = jnp.sum(values * values, axis=-1, keepdims=True) * (1.0 / width)
        normed = values * lax.rsqrt(mean_square + 1e-06) * gain_ref[...]
        normed = normed.astype(jnp.bfloat16)
        for t in range(copies_ref.shape[0]):
            copies_ref[t, b] = normed


def pack_body(in_ref, out_ref, o_ref):
    units, part = in_ref.shape
    o_ref[:units, :part] = in_ref[...]
    o_ref[units:, :part] = out_ref[...]
    o_ref[:, part:] = jnp.zeros((2 * units, LANE - part), o_ref.dtype)


def mlp_body(part, chunks, x_ref, w_ref, o_ref, held, sems):
    sections, both, _ = w_ref.shape
    units = both // 2
    size = sections // chunks
    copies = []
    for half in range(2):
        for c in range(chunks):
            place = (pl.ds(c * size, size), pl.ds(half * units, units))
            copy = pltpu.make_async_copy(w_ref.at[place], held.at[place], sems.at[half, c])
            copy.start()
            copies.append(copy)
    total = jnp.zeros((x_ref.shape[0], units), jnp.float32)
    for s in range(sections):
        if s % size == 0:
            copies[s // size].wait()
        total += lax.dot_general(
            x_ref[:, s * part : (s + 1) * part],
            held[s, :units, :part],
            (((1,), (1,)), ((), ())),
            preferred_element_type=jnp.float32,
        )
    hidden = 0.5 * total * (1.0 + lax.erf(total * (0.5**0.5)))
    hidden = hidden.astype(jnp.bfloat16)
    for s in range(sections):
        if s % size == 0:
            copies[chunks + s // size].wait()
        o_ref[:, s * part : (s + 1) * part] = jnp.dot(
            hidden, held[s, units:, :part], preferred_element_type=jnp.float32
        ).astype(jnp.bfloat16)


def sum_body(x_ref, rows_ref, scale_ref, o_ref):
    blocks = rows_ref.shape[0]
    for b in range(blocks):
        branch = x_ref[0, b].astype(jnp.float32)
        for t in range(1, x_ref.shape[0]):
            branch += x_ref[t, b].astype(jnp.float32)
        values = rows_ref[b].astype(jnp.float32)
        o_ref[b] = (values + scale_ref[...] * branch).astype(o_ref.dtype)


def local(sections, groups, patches, plan, norm_gain, proj_in, proj_out, layer_scale):
    blocks, rows, width = patches.shape
    bf16 = jnp.bfloat16
    part, units = proj_in.shape
    weights = call(pack_body, jax.ShapeDtypeStruct((2 * units, LANE), bf16), [VMEM, VMEM])(
        proj_in.T, proj_out
    )
    weights = lax.all_gather(weights, "section", axis=0, tiled=False)

    shape = jax.ShapeDtypeStruct((sections * blocks, rows, LANE), bf16)
    tiles = call(split_body, shape, [VMEM])(patches)
    tiles = lax.all_to_all(tiles, "section", 0, 0, tiled=True)
    tiles = call(order_body, shape, [SMEM, VMEM])(plan, tiles)
    tiles = lax.all_to_all(tiles, "section", 0, 0, tiled=True)
    own, copies = call(
        norm_body,
        (
            jax.ShapeDtypeStruct((blocks, rows, width), bf16),
            jax.ShapeDtypeStruct((groups, blocks, rows, width), bf16),
        ),
        [VMEM, VMEM],
        n_out=2,
    )(tiles, norm_gain.reshape(1, width))

    all_rows = groups * blocks * rows
    normed = lax.all_to_all(copies.reshape(all_rows, width), "tensor", 0, 0, tiled=True)
    chunks = 4
    partial_sum = call(
        functools.partial(mlp_body, part, chunks),
        jax.ShapeDtypeStruct((all_rows, width), bf16),
        [VMEM, pl.BlockSpec(memory_space=pltpu.HBM)],
        flops=4 * all_rows * width * units,
        moved=10 * 1024 * 1024,
        scratch=[
            pltpu.VMEM((sections, 2 * units, LANE), bf16),
            pltpu.SemaphoreType.DMA((2, chunks)),
        ],
    )(normed, weights)
    terms = lax.all_to_all(partial_sum, "tensor", 0, 0, tiled=True)
    return call(
        sum_body, jax.ShapeDtypeStruct((blocks, rows, width), bf16), [VMEM, VMEM, VMEM]
    )(terms.reshape(groups, blocks, rows, width), own, layer_scale.reshape(1, width))


def solution(mesh):
    return jax.shard_map(
        functools.partial(local, mesh.shape["section"], mesh.shape["tensor"]),
        mesh=mesh,
        in_specs=(
            P("section", "tensor", None),
            P(),
            P(),
            P("section", "tensor"),
            P("tensor", "section"),
            P(),
        ),
        out_specs=P("section", "tensor", None),
        check_vma=False,
    )
```

```python
import functools

import jax
import jax.numpy as jnp
from jax import lax
from jax.experimental import pallas as pl
from jax.experimental.pallas import tpu as pltpu
from jax.sharding import PartitionSpec as P

LANE = 128
VMEM = pl.BlockSpec(memory_space=pltpu.VMEM)
ANY = pl.BlockSpec(memory_space=pl.ANY)
SMEM = pl.BlockSpec(memory_space=pltpu.SMEM)


def call(body, out_shape, in_specs, flops=0, moved=0, n_out=1, scratch=()):
    return pl.pallas_call(
        body,
        out_shape=out_shape,
        in_specs=in_specs,
        out_specs=VMEM if n_out == 1 else [VMEM] * n_out,
        scratch_shapes=list(scratch),
        compiler_params=pltpu.CompilerParams(vmem_limit_bytes=32 * 1024 * 1024),
        cost_estimate=pl.CostEstimate(flops=flops, bytes_accessed=moved, transcendentals=0),
    )


def split_body(x_ref, o_ref):
    blocks, rows, width = x_ref.shape
    for m in range(o_ref.shape[0] // blocks):
        if (m + 1) * LANE <= width:
            for b in range(blocks):
                o_ref[m * blocks + b] = x_ref[b, :, m * LANE : (m + 1) * LANE]
        else:
            for b in range(blocks):
                o_ref[m * blocks + b] = jnp.zeros((rows, LANE), o_ref.dtype)


def order_body(plan_ref, x_ref, *refs):
    o_ref = refs[-1]
    for p in range(o_ref.shape[0]):
        o_ref[p] = x_ref[plan_ref[p]]


def norm_body(x_ref, gain_ref, *refs):
    rows_ref, copies_ref = refs[-2:]
    blocks, rows, width = rows_ref.shape
    tiles = width // LANE
    for b in range(blocks):
        whole = jnp.concatenate([x_ref[m * blocks + b] for m in range(tiles)], axis=-1)
        rows_ref[b] = whole
        values = whole.astype(jnp.float32)
        mean_square = jnp.sum(values * values, axis=-1, keepdims=True) * (1.0 / width)
        normed = values * lax.rsqrt(mean_square + 1e-06) * gain_ref[...]
        normed = normed.astype(jnp.bfloat16)
        for t in range(copies_ref.shape[0]):
            copies_ref[t, b] = normed


def pack_body(in_ref, out_ref, o_ref):
    units, part = in_ref.shape
    o_ref[:units, :part] = in_ref[...]
    o_ref[units:, :part] = out_ref[...]
    o_ref[:, part:] = jnp.zeros((2 * units, LANE - part), o_ref.dtype)


def mlp_body(part, offsets, sizes, x_ref, *refs):
    n = len(offsets)
    mine, others = refs[:n], refs[n : n + len(sizes)]
    o_ref, held, sems = refs[n + len(sizes) :]
    sections, both, _ = held.shape
    units = both // 2
    me = lax.axis_index("section")
    core = lax.rem(me, 2)
    shards = list(mine)
    for ref, size in zip(others, sizes):
        shards += [ref.at[k] for k in range(size)]
    copies = []
    for half in range(2):
        rows = pl.ds(half * units, units)
        for k, shard in enumerate(shards):
            ring = lax.rem(me - core + 2 * offsets[k % n] + 2 * sections, sections)
            place = ring + (core if k < n else 1 - core)
            copy = pltpu.make_async_copy(shard.at[rows], held.at[place, rows], sems.at[half, k])
            copy.start()
            copies.append(copy)
    for copy in copies[: 2 * n]:
        copy.wait()
    total = jnp.zeros((x_ref.shape[0], units), jnp.float32)
    for s in range(sections):
        total += lax.dot_general(
            x_ref[:, s * part : (s + 1) * part],
            held[s, :units, :part],
            (((1,), (1,)), ((), ())),
            preferred_element_type=jnp.float32,
        )
    hidden = 0.5 * total * (1.0 + lax.erf(total * (0.5**0.5)))
    hidden = hidden.astype(jnp.bfloat16)
    for copy in copies[2 * n :]:
        copy.wait()
    for s in range(sections):
        o_ref[:, s * part : (s + 1) * part] = jnp.dot(
            hidden, held[s, units:, :part], preferred_element_type=jnp.float32
        ).astype(jnp.bfloat16)


def shifted(x, sections, steps):
    return lax.ppermute(x, "section", [(i, (i + 2 * steps) % sections) for i in range(sections)])


def gather_weights(mine, sections):
    chips = sections // 2
    ahead, back = chips // 2, (chips - 1) // 2
    swap = [(i, i ^ 1) for i in range(sections)]
    shards, offsets, groups, sizes = [mine], [0], [], []
    down, up = mine, mine
    done = 0
    for step in range(1, ahead + 1):
        down = shifted(down, sections, 1)
        shards.append(down)
        offsets.append(-step)
        if step <= back:
            up = shifted(up, sections, -1)
            shards.append(up)
            offsets.append(step)
        if step in (3, 6, ahead):
            group = jnp.stack(shards[done:])
            groups.append(lax.ppermute(group, "section", swap))
            sizes.append(len(shards) - done)
            done = len(shards)
    return shards, offsets, groups, sizes


def sum_body(x_ref, rows_ref, scale_ref, o_ref):
    blocks = rows_ref.shape[0]
    for b in range(blocks):
        branch = x_ref[0, b].astype(jnp.float32)
        for t in range(1, x_ref.shape[0]):
            branch += x_ref[t, b].astype(jnp.float32)
        values = rows_ref[b].astype(jnp.float32)
        o_ref[b] = (values + scale_ref[...] * branch).astype(o_ref.dtype)


def local(sections, groups, patches, plan, norm_gain, proj_in, proj_out, layer_scale):
    blocks, rows, width = patches.shape
    bf16 = jnp.bfloat16
    part, units = proj_in.shape
    weights = call(pack_body, jax.ShapeDtypeStruct((2 * units, LANE), bf16), [VMEM, VMEM])(
        proj_in.T, proj_out
    )
    shards, offsets, others, sizes = gather_weights(weights, sections)

    shape = jax.ShapeDtypeStruct((sections * blocks, rows, LANE), bf16)
    tiles = call(split_body, shape, [VMEM])(patches)
    tiles = lax.all_to_all(tiles, "section", 0, 0, tiled=True)
    first, second = shards[3:5], shards[9:11]
    tiles = call(order_body, shape, [SMEM, VMEM, ANY, ANY])(plan, tiles, *first)
    tiles = lax.all_to_all(tiles, "section", 0, 0, tiled=True)
    own, copies = call(
        norm_body,
        (
            jax.ShapeDtypeStruct((blocks, rows, width), bf16),
            jax.ShapeDtypeStruct((groups, blocks, rows, width), bf16),
        ),
        [VMEM, VMEM, ANY, ANY],
        n_out=2,
    )(tiles, norm_gain.reshape(1, width), *second)

    all_rows = groups * blocks * rows
    normed = lax.all_to_all(copies.reshape(all_rows, width), "tensor", 0, 0, tiled=True)
    partial_sum = call(
        functools.partial(mlp_body, part, offsets, sizes),
        jax.ShapeDtypeStruct((all_rows, width), bf16),
        [VMEM] + [ANY] * (len(shards) + len(others)),
        flops=4 * all_rows * width * units,
        moved=10 * 1024 * 1024,
        scratch=[
            pltpu.VMEM((sections, 2 * units, LANE), bf16),
            pltpu.SemaphoreType.DMA((2, sections)),
        ],
    )(normed, *shards, *others)
    terms = lax.all_to_all(partial_sum, "tensor", 0, 0, tiled=True)
    return call(
        sum_body, jax.ShapeDtypeStruct((blocks, rows, width), bf16), [VMEM, VMEM, VMEM]
    )(terms.reshape(groups, blocks, rows, width), own, layer_scale.reshape(1, width))


def solution(mesh):
    return jax.shard_map(
        functools.partial(local, mesh.shape["section"], mesh.shape["tensor"]),
        mesh=mesh,
        in_specs=(
            P("section", "tensor", None),
            P(),
            P(),
            P("section", "tensor"),
            P("tensor", "section"),
            P(),
        ),
        out_specs=P("section", "tensor", None),
        check_vma=False,
    )
```

```python
import functools

import jax
import jax.numpy as jnp
from jax import lax
from jax.experimental import pallas as pl
from jax.experimental.pallas import tpu as pltpu
from jax.sharding import PartitionSpec as P

LANE = 128
VMEM = pl.BlockSpec(memory_space=pltpu.VMEM)
ANY = pl.BlockSpec(memory_space=pl.ANY)
SMEM = pl.BlockSpec(memory_space=pltpu.SMEM)


def call(body, out_shape, in_specs, flops=0, moved=0, n_out=1, scratch=(), limit=32):
    return pl.pallas_call(
        body,
        out_shape=out_shape,
        in_specs=in_specs,
        out_specs=VMEM if n_out == 1 else [VMEM] * n_out,
        scratch_shapes=list(scratch),
        compiler_params=pltpu.CompilerParams(vmem_limit_bytes=limit * 1024 * 1024),
        cost_estimate=pl.CostEstimate(flops=flops, bytes_accessed=moved, transcendentals=0),
    )


def split_body(x_ref, o_ref):
    blocks, rows, width = x_ref.shape
    for m in range(o_ref.shape[0] // blocks):
        if (m + 1) * LANE <= width:
            for b in range(blocks):
                o_ref[m * blocks + b] = x_ref[b, :, m * LANE : (m + 1) * LANE]
        else:
            for b in range(blocks):
                o_ref[m * blocks + b] = jnp.zeros((rows, LANE), o_ref.dtype)


def order_body(plan_ref, x_ref, o_ref):
    for p in range(o_ref.shape[0]):
        o_ref[p] = x_ref[plan_ref[p]]


def norm_body(x_ref, gain_ref, rows_ref, copies_ref):
    blocks, rows, width = rows_ref.shape
    tiles = width // LANE
    for b in range(blocks):
        whole = jnp.concatenate([x_ref[m * blocks + b] for m in range(tiles)], axis=-1)
        rows_ref[b] = whole
        values = whole.astype(jnp.float32)
        mean_square = jnp.sum(values * values, axis=-1, keepdims=True) * (1.0 / width)
        normed = values * lax.rsqrt(mean_square + 1e-06) * gain_ref[...]
        normed = normed.astype(jnp.bfloat16)
        for t in range(copies_ref.shape[0]):
            copies_ref[t, b] = normed


def pack_body(in_ref, out_ref, o_ref):
    part = in_ref.shape[1]
    kept = o_ref.shape[0] // 2
    fold, chunk = kept // 4, part // 4
    for k, ref in enumerate((in_ref, out_ref)):
        at = k * kept
        o_ref[at : at + kept, :part] = ref[:kept, :]
        for j in range(4):
            o_ref[at + j * fold : at + (j + 1) * fold, part : part + chunk] = ref[
                kept:, j * chunk : (j + 1) * chunk
            ]
        o_ref[at : at + kept, part + chunk :] = jnp.zeros((kept, LANE - part - chunk), o_ref.dtype)


def unpacked(packed, part):
    fold, chunk = packed.shape[0] // 4, part // 4
    rest = [packed[j * fold : (j + 1) * fold, part : part + chunk] for j in range(4)]
    return jnp.concatenate([packed[:, :part], jnp.concatenate(rest, axis=1)], axis=0)


def mlp_body(part, units, chunks, x_hbm, w_hbm, o_ref, x_ref, held, x_sem, sems):
    sections, both, _ = held.shape
    kept = both // 2
    size = sections // chunks
    x_copy = pltpu.make_async_copy(x_hbm, x_ref, x_sem)
    x_copy.start()
    copies = []
    for half in range(2):
        for c in range(chunks):
            place = (pl.ds(c * size, size), pl.ds(half * kept, kept))
            copy = pltpu.make_async_copy(w_hbm.at[place], held.at[place], sems.at[half, c])
            copy.start()
            copies.append(copy)
    x_copy.wait()
    total = jnp.zeros((x_ref.shape[0], units), jnp.float32)
    for s in range(sections):
        if s % size == 0:
            copies[s // size].wait()
        total += lax.dot_general(
            x_ref[:, s * part : (s + 1) * part],
            unpacked(held[s, :kept, :], part),
            (((1,), (1,)), ((), ())),
            preferred_element_type=jnp.float32,
        )
    hidden = 0.5 * total * (1.0 + lax.erf(total * (0.5**0.5)))
    hidden = hidden.astype(jnp.bfloat16)
    for s in range(sections):
        if s % size == 0:
            copies[chunks + s // size].wait()
        o_ref[:, s * part : (s + 1) * part] = jnp.dot(
            hidden, unpacked(held[s, kept:, :], part), preferred_element_type=jnp.float32
        ).astype(jnp.bfloat16)


def sum_body(x_ref, rows_ref, scale_ref, o_ref):
    blocks = rows_ref.shape[0]
    for b in range(blocks):
        branch = x_ref[0, b].astype(jnp.float32)
        for t in range(1, x_ref.shape[0]):
            branch += x_ref[t, b].astype(jnp.float32)
        values = rows_ref[b].astype(jnp.float32)
        o_ref[b] = (values + scale_ref[...] * branch).astype(o_ref.dtype)


def local(sections, groups, patches, plan, norm_gain, proj_in, proj_out, layer_scale):
    blocks, rows, width = patches.shape
    bf16 = jnp.bfloat16
    part, units = proj_in.shape
    kept = units * 4 // 5
    weights = call(
        pack_body, jax.ShapeDtypeStruct((2 * kept, LANE), bf16), [VMEM, VMEM], limit=60
    )(proj_in.T, proj_out)
    weights = lax.all_gather(weights, "section", axis=0, tiled=False)

    shape = jax.ShapeDtypeStruct((sections * blocks, rows, LANE), bf16)
    tiles = call(split_body, shape, [VMEM])(patches)
    tiles = lax.all_to_all(tiles, "section", 0, 0, tiled=True)
    tiles = call(order_body, shape, [SMEM, VMEM])(plan, tiles)
    tiles = lax.all_to_all(tiles, "section", 0, 0, tiled=True)
    own, copies = call(
        norm_body,
        (
            jax.ShapeDtypeStruct((blocks, rows, width), bf16),
            jax.ShapeDtypeStruct((groups, blocks, rows, width), bf16),
        ),
        [VMEM, VMEM],
        n_out=2,
    )(tiles, norm_gain.reshape(1, width))

    all_rows = groups * blocks * rows
    normed = lax.all_to_all(copies.reshape(all_rows, width), "tensor", 0, 0, tiled=True)
    chunks = 4
    partial_sum = call(
        functools.partial(mlp_body, part, units, chunks),
        jax.ShapeDtypeStruct((all_rows, width), bf16),
        [ANY, ANY],
        flops=4 * all_rows * width * units,
        moved=10 * 1024 * 1024,
        scratch=[
            pltpu.VMEM((all_rows, width), bf16),
            pltpu.VMEM((sections, 2 * kept, LANE), bf16),
            pltpu.SemaphoreType.DMA(()),
            pltpu.SemaphoreType.DMA((2, chunks)),
        ],
        limit=60,
    )(normed, weights)
    terms = lax.all_to_all(partial_sum, "tensor", 0, 0, tiled=True)
    return call(
        sum_body, jax.ShapeDtypeStruct((blocks, rows, width), bf16), [VMEM, VMEM, VMEM]
    )(terms.reshape(groups, blocks, rows, width), own, layer_scale.reshape(1, width))


def solution(mesh):
    return jax.shard_map(
        functools.partial(local, mesh.shape["section"], mesh.shape["tensor"]),
        mesh=mesh,
        in_specs=(
            P("section", "tensor", None),
            P(),
            P(),
            P("section", "tensor"),
            P("tensor", "section"),
            P(),
        ),
        out_specs=P("section", "tensor", None),
        check_vma=False,
    )
```

```python
import functools

import jax
import jax.numpy as jnp
from jax import lax
from jax.experimental import pallas as pl
from jax.experimental.pallas import tpu as pltpu
from jax.sharding import PartitionSpec as P

LANE = 128
VMEM = pl.BlockSpec(memory_space=pltpu.VMEM)
ANY = pl.BlockSpec(memory_space=pl.ANY)
SMEM = pl.BlockSpec(memory_space=pltpu.SMEM)


def call(body, out_shape, in_specs, flops=0, moved=0, n_out=1, scratch=(), limit=32):
    return pl.pallas_call(
        body,
        out_shape=out_shape,
        in_specs=in_specs,
        out_specs=VMEM if n_out == 1 else [VMEM] * n_out,
        scratch_shapes=list(scratch),
        compiler_params=pltpu.CompilerParams(vmem_limit_bytes=limit * 1024 * 1024),
        cost_estimate=pl.CostEstimate(flops=flops, bytes_accessed=moved, transcendentals=0),
    )


def split_body(x_ref, o_ref):
    blocks, rows, width = x_ref.shape
    for m in range(o_ref.shape[0] // blocks):
        if (m + 1) * LANE <= width:
            for b in range(blocks):
                o_ref[m * blocks + b] = x_ref[b, :, m * LANE : (m + 1) * LANE]
        else:
            for b in range(blocks):
                o_ref[m * blocks + b] = jnp.zeros((rows, LANE), o_ref.dtype)


def order_body(plan_ref, x_ref, o_ref):
    for p in range(o_ref.shape[0]):
        o_ref[p] = x_ref[plan_ref[p]]


def norm_body(x_ref, gain_ref, rows_ref, copies_ref):
    blocks, rows, width = rows_ref.shape
    tiles = width // LANE
    for b in range(blocks):
        whole = jnp.concatenate([x_ref[m * blocks + b] for m in range(tiles)], axis=-1)
        rows_ref[b] = whole
        values = whole.astype(jnp.float32)
        mean_square = jnp.sum(values * values, axis=-1, keepdims=True) * (1.0 / width)
        normed = values * lax.rsqrt(mean_square + 1e-06) * gain_ref[...]
        normed = normed.astype(jnp.bfloat16)
        for t in range(copies_ref.shape[0]):
            copies_ref[t, b] = normed


def pack_body(in_ref, out_ref, o_ref):
    units, part = in_ref.shape
    o_ref[:units, :part] = in_ref[...]
    o_ref[units:, :part] = out_ref[...]
    o_ref[:, part:] = jnp.zeros((2 * units, LANE - part), o_ref.dtype)


def mlp_body(part, x_hbm, w_hbm, o_ref, x_ref, spread, held, x_sem, in_sem, out_sem):
    sections, both, _ = held.shape
    units = both // 2
    rows = x_ref.shape[0]
    x_copy = pltpu.make_async_copy(x_hbm, x_ref, x_sem)
    x_copy.start()
    first, second = pl.ds(0, units), pl.ds(units, units)
    in_copy = pltpu.make_async_copy(w_hbm.at[:, first], held.at[:, first], in_sem)
    in_copy.start()
    out_copy = pltpu.make_async_copy(w_hbm.at[:, second], held.at[:, second], out_sem)
    out_copy.start()
    x_copy.wait()
    blank = jnp.zeros((rows, LANE - part), x_ref.dtype)
    for s in range(sections):
        spread[:, s * LANE : (s + 1) * LANE] = jnp.concatenate(
            [x_ref[:, s * part : (s + 1) * part], blank], axis=1
        )
    in_copy.wait()
    total = jnp.zeros((rows, units), jnp.float32)
    for s in range(0, sections, 2):
        total += lax.dot_general(
            spread[:, s * LANE : (s + 2) * LANE],
            jnp.concatenate([held[s, :units, :], held[s + 1, :units, :]], axis=1),
            (((1,), (1,)), ((), ())),
            preferred_element_type=jnp.float32,
        )
    hidden = 0.5 * total * (1.0 + lax.erf(total * (0.5**0.5)))
    hidden = hidden.astype(jnp.bfloat16)
    out_copy.wait()
    for s in range(0, sections, 2):
        product = jnp.dot(
            hidden,
            jnp.concatenate([held[s, units:, :], held[s + 1, units:, :]], axis=1),
            preferred_element_type=jnp.float32,
        ).astype(jnp.bfloat16)
        for i in range(2):
            o_ref[:, (s + i) * part : (s + i + 1) * part] = product[:, i * LANE : i * LANE + part]


def sum_body(x_ref, rows_ref, scale_ref, o_ref):
    blocks = rows_ref.shape[0]
    for b in range(blocks):
        branch = x_ref[0, b].astype(jnp.float32)
        for t in range(1, x_ref.shape[0]):
            branch += x_ref[t, b].astype(jnp.float32)
        values = rows_ref[b].astype(jnp.float32)
        o_ref[b] = (values + scale_ref[...] * branch).astype(o_ref.dtype)


def local(sections, groups, patches, plan, norm_gain, proj_in, proj_out, layer_scale):
    blocks, rows, width = patches.shape
    bf16 = jnp.bfloat16
    part, units = proj_in.shape
    weights = call(
        pack_body, jax.ShapeDtypeStruct((2 * units, LANE), bf16), [VMEM, VMEM], limit=60
    )(proj_in.T, proj_out)
    weights = lax.all_gather(weights, "section", axis=0, tiled=False)

    shape = jax.ShapeDtypeStruct((sections * blocks, rows, LANE), bf16)
    tiles = call(split_body, shape, [VMEM])(patches)
    tiles = lax.all_to_all(tiles, "section", 0, 0, tiled=True)
    tiles = call(order_body, shape, [SMEM, VMEM])(plan, tiles)
    tiles = lax.all_to_all(tiles, "section", 0, 0, tiled=True)
    own, copies = call(
        norm_body,
        (
            jax.ShapeDtypeStruct((blocks, rows, width), bf16),
            jax.ShapeDtypeStruct((groups, blocks, rows, width), bf16),
        ),
        [VMEM, VMEM],
        n_out=2,
    )(tiles, norm_gain.reshape(1, width))

    all_rows = groups * blocks * rows
    normed = lax.all_to_all(copies.reshape(all_rows, width), "tensor", 0, 0, tiled=True)
    partial_sum = call(
        functools.partial(mlp_body, part),
        jax.ShapeDtypeStruct((all_rows, width), bf16),
        [ANY, ANY],
        flops=4 * all_rows * width * units,
        moved=10 * 1024 * 1024,
        scratch=[
            pltpu.VMEM((all_rows, width), bf16),
            pltpu.VMEM((all_rows, sections * LANE), bf16),
            pltpu.VMEM((sections, 2 * units, LANE), bf16),
            pltpu.SemaphoreType.DMA(()),
            pltpu.SemaphoreType.DMA(()),
            pltpu.SemaphoreType.DMA(()),
        ],
        limit=60,
    )(normed, weights)
    terms = lax.all_to_all(partial_sum, "tensor", 0, 0, tiled=True)
    return call(
        sum_body, jax.ShapeDtypeStruct((blocks, rows, width), bf16), [VMEM, VMEM, VMEM]
    )(terms.reshape(groups, blocks, rows, width), own, layer_scale.reshape(1, width))


def solution(mesh):
    return jax.shard_map(
        functools.partial(local, mesh.shape["section"], mesh.shape["tensor"]),
        mesh=mesh,
        in_specs=(
            P("section", "tensor", None),
            P(),
            P(),
            P("section", "tensor"),
            P("tensor", "section"),
            P(),
        ),
        out_specs=P("section", "tensor", None),
        check_vma=False,
    )
```

```python
import functools

import jax
import jax.numpy as jnp
from jax import lax
from jax.experimental import pallas as pl
from jax.experimental.pallas import tpu as pltpu
from jax.sharding import PartitionSpec as P

LANE = 128
VMEM = pl.BlockSpec(memory_space=pltpu.VMEM)
ANY = pl.BlockSpec(memory_space=pl.ANY)
SMEM = pl.BlockSpec(memory_space=pltpu.SMEM)


def call(body, out_shape, in_specs, flops=0, moved=0, n_out=1, scratch=(), limit=32):
    return pl.pallas_call(
        body,
        out_shape=out_shape,
        in_specs=in_specs,
        out_specs=VMEM if n_out == 1 else [VMEM] * n_out,
        scratch_shapes=list(scratch),
        compiler_params=pltpu.CompilerParams(vmem_limit_bytes=limit * 1024 * 1024),
        cost_estimate=pl.CostEstimate(flops=flops, bytes_accessed=moved, transcendentals=0),
    )


def first_body(x_ref, in_ref, out_ref, weights_ref, tiles_ref):
    units, part = in_ref.shape
    weights_ref[:units, :part] = in_ref[...]
    weights_ref[units:, :part] = out_ref[...]
    weights_ref[:, part:] = jnp.zeros((2 * units, LANE - part), weights_ref.dtype)
    blocks, rows, width = x_ref.shape
    for m in range(tiles_ref.shape[0] // blocks):
        for b in range(blocks):
            if (m + 1) * LANE <= width:
                tiles_ref[m * blocks + b] = x_ref[b, :, m * LANE : (m + 1) * LANE]
            else:
                tiles_ref[m * blocks + b] = jnp.zeros((rows, LANE), tiles_ref.dtype)


def order_body(plan_ref, x_ref, o_ref):
    for p in range(o_ref.shape[0]):
        o_ref[p] = x_ref[plan_ref[p]]


def norm_body(x_ref, gain_ref, rows_ref, copies_ref):
    blocks, rows, width = rows_ref.shape
    tiles = width // LANE
    for b in range(blocks):
        whole = jnp.concatenate([x_ref[m * blocks + b] for m in range(tiles)], axis=-1)
        rows_ref[b] = whole
        values = whole.astype(jnp.float32)
        mean_square = jnp.sum(values * values, axis=-1, keepdims=True) * (1.0 / width)
        normed = values * lax.rsqrt(mean_square + 1e-06) * gain_ref[...].reshape(1, width)
        normed = normed.astype(jnp.bfloat16)
        for t in range(copies_ref.shape[0]):
            copies_ref[t, b] = normed


def mlp_body(part, x_hbm, w_hbm, o_ref, x_ref, spread, held, x_sem, in_sem, out_sem):
    sections, both, _ = held.shape
    units = both // 2
    rows = x_ref.shape[0]
    x_copy = pltpu.make_async_copy(x_hbm, x_ref, x_sem)
    x_copy.start()
    first, second = pl.ds(0, units), pl.ds(units, units)
    in_copy = pltpu.make_async_copy(w_hbm.at[:, first], held.at[:, first], in_sem)
    in_copy.start()
    out_copy = pltpu.make_async_copy(w_hbm.at[:, second], held.at[:, second], out_sem)
    out_copy.start()
    x_copy.wait()
    blank = jnp.zeros((rows, LANE - part), x_ref.dtype)
    for s in range(sections):
        spread[:, s * LANE : (s + 1) * LANE] = jnp.concatenate(
            [x_ref[:, s * part : (s + 1) * part], blank], axis=1
        )
    in_copy.wait()
    total = jnp.zeros((rows, units), jnp.float32)
    for s in range(0, sections, 2):
        total += lax.dot_general(
            spread[:, s * LANE : (s + 2) * LANE],
            jnp.concatenate([held[s, :units, :], held[s + 1, :units, :]], axis=1),
            (((1,), (1,)), ((), ())),
            preferred_element_type=jnp.float32,
        )
    hidden = 0.5 * total * (1.0 + lax.erf(total * (0.5**0.5)))
    hidden = hidden.astype(jnp.bfloat16)
    out_copy.wait()
    for s in range(0, sections, 2):
        product = jnp.dot(
            hidden,
            jnp.concatenate([held[s, units:, :], held[s + 1, units:, :]], axis=1),
            preferred_element_type=jnp.float32,
        ).astype(jnp.bfloat16)
        for i in range(2):
            o_ref[:, (s + i) * part : (s + i + 1) * part] = product[:, i * LANE : i * LANE + part]


def sum_body(x_ref, rows_ref, scale_ref, o_ref):
    blocks = rows_ref.shape[0]
    for b in range(blocks):
        branch = x_ref[0, b].astype(jnp.float32)
        for t in range(1, x_ref.shape[0]):
            branch += x_ref[t, b].astype(jnp.float32)
        values = rows_ref[b].astype(jnp.float32)
        o_ref[b] = (values + scale_ref[...].reshape(1, -1) * branch).astype(o_ref.dtype)


def local(sections, groups, patches, plan, norm_gain, proj_in, proj_out, layer_scale):
    blocks, rows, width = patches.shape
    bf16 = jnp.bfloat16
    part, units = proj_in.shape
    shape = jax.ShapeDtypeStruct((sections * blocks, rows, LANE), bf16)
    weights, tiles = call(
        first_body,
        (jax.ShapeDtypeStruct((2 * units, LANE), bf16), shape),
        [VMEM, VMEM, VMEM],
        n_out=2,
        limit=60,
    )(patches, proj_in.T, proj_out)
    weights = lax.all_gather(weights, "section", axis=0, tiled=False)
    tiles = lax.all_to_all(tiles, "section", 0, 0, tiled=True)
    tiles = call(order_body, shape, [SMEM, VMEM], limit=60)(plan, tiles)
    tiles = lax.all_to_all(tiles, "section", 0, 0, tiled=True)
    own, copies = call(
        norm_body,
        (
            jax.ShapeDtypeStruct((blocks, rows, width), bf16),
            jax.ShapeDtypeStruct((groups, blocks, rows, width), bf16),
        ),
        [VMEM, VMEM],
        n_out=2,
        limit=60,
    )(tiles, norm_gain)

    all_rows = groups * blocks * rows
    normed = lax.all_to_all(copies.reshape(all_rows, width), "tensor", 0, 0, tiled=True)
    partial_sum = call(
        functools.partial(mlp_body, part),
        jax.ShapeDtypeStruct((all_rows, width), bf16),
        [ANY, ANY],
        flops=4 * all_rows * width * units,
        moved=10 * 1024 * 1024,
        scratch=[
            pltpu.VMEM((all_rows, width), bf16),
            pltpu.VMEM((all_rows, sections * LANE), bf16),
            pltpu.VMEM((sections, 2 * units, LANE), bf16),
            pltpu.SemaphoreType.DMA(()),
            pltpu.SemaphoreType.DMA(()),
            pltpu.SemaphoreType.DMA(()),
        ],
        limit=60,
    )(normed, weights)
    terms = lax.all_to_all(partial_sum, "tensor", 0, 0, tiled=True)
    return call(
        sum_body,
        jax.ShapeDtypeStruct((blocks, rows, width), bf16),
        [VMEM, VMEM, VMEM],
        limit=60,
    )(terms.reshape(groups, blocks, rows, width), own, layer_scale)


def solution(mesh):
    return jax.shard_map(
        functools.partial(local, mesh.shape["section"], mesh.shape["tensor"]),
        mesh=mesh,
        in_specs=(
            P("section", "tensor", None),
            P(),
            P(),
            P("section", "tensor"),
            P("tensor", "section"),
            P(),
        ),
        out_specs=P("section", "tensor", None),
        check_vma=False,
    )
```

```python
import functools

import jax
import jax.numpy as jnp
from jax import lax
from jax.experimental import pallas as pl
from jax.experimental.pallas import tpu as pltpu
from jax.sharding import PartitionSpec as P

LANE = 128
VMEM = pl.BlockSpec(memory_space=pltpu.VMEM)
ANY = pl.BlockSpec(memory_space=pl.ANY)
SMEM = pl.BlockSpec(memory_space=pltpu.SMEM)


def call(body, out_shape, in_specs, flops=0, moved=0, n_out=1, scratch=(), limit=32):
    return pl.pallas_call(
        body,
        out_shape=out_shape,
        in_specs=in_specs,
        out_specs=VMEM if n_out == 1 else [VMEM] * n_out,
        scratch_shapes=list(scratch),
        compiler_params=pltpu.CompilerParams(vmem_limit_bytes=limit * 1024 * 1024),
        cost_estimate=pl.CostEstimate(flops=flops, bytes_accessed=moved, transcendentals=0),
    )


def first_body(x_ref, in_ref, out_ref, weights_ref, tiles_ref):
    units, part = in_ref.shape
    weights_ref[:units, :part] = in_ref[...]
    weights_ref[units:, :part] = out_ref[...]
    weights_ref[:, part:] = jnp.zeros((2 * units, LANE - part), weights_ref.dtype)
    blocks, rows, width = x_ref.shape
    for m in range(tiles_ref.shape[0] // blocks):
        for b in range(blocks):
            if (m + 1) * LANE <= width:
                tiles_ref[m * blocks + b] = x_ref[b, :, m * LANE : (m + 1) * LANE]
            else:
                tiles_ref[m * blocks + b] = jnp.zeros((rows, LANE), tiles_ref.dtype)


def order_body(plan_ref, x_ref, o_ref):
    for p in range(o_ref.shape[0]):
        o_ref[p] = x_ref[plan_ref[p]]


def norm_body(x_ref, gain_ref, rows_ref, copies_ref):
    blocks, rows, width = rows_ref.shape
    tiles = width // LANE
    for b in range(blocks):
        whole = jnp.concatenate([x_ref[m * blocks + b] for m in range(tiles)], axis=-1)
        rows_ref[b] = whole
        values = whole.astype(jnp.float32)
        mean_square = jnp.sum(values * values, axis=-1, keepdims=True) * (1.0 / width)
        normed = values * lax.rsqrt(mean_square + 1e-06) * gain_ref[...].reshape(1, width)
        normed = normed.astype(jnp.bfloat16)
        for t in range(copies_ref.shape[0]):
            copies_ref[t, b] = normed


def mlp_body(part, x_hbm, w_hbm, scale_ref, o_ref, x_ref, spread, held, x_sem, in_sem, out_sem):
    sections, both, _ = held.shape
    units = both // 2
    rows = x_ref.shape[0]
    x_copy = pltpu.make_async_copy(x_hbm, x_ref, x_sem)
    x_copy.start()
    first, second = pl.ds(0, units), pl.ds(units, units)
    in_copy = pltpu.make_async_copy(w_hbm.at[:, first], held.at[:, first], in_sem)
    in_copy.start()
    out_copy = pltpu.make_async_copy(w_hbm.at[:, second], held.at[:, second], out_sem)
    out_copy.start()
    x_copy.wait()
    blank = jnp.zeros((rows, LANE - part), x_ref.dtype)
    for s in range(sections):
        spread[:, s * LANE : (s + 1) * LANE] = jnp.concatenate(
            [x_ref[:, s * part : (s + 1) * part], blank], axis=1
        )
    in_copy.wait()
    total = jnp.zeros((rows, units), jnp.float32)
    for s in range(0, sections, 2):
        total += lax.dot_general(
            spread[:, s * LANE : (s + 2) * LANE],
            jnp.concatenate([held[s, :units, :], held[s + 1, :units, :]], axis=1),
            (((1,), (1,)), ((), ())),
            preferred_element_type=jnp.float32,
        )
    hidden = 0.5 * total * (1.0 + lax.erf(total * (0.5**0.5)))
    hidden = hidden.astype(jnp.bfloat16)
    scale = scale_ref[...].reshape(1, sections * part)
    edge = jnp.zeros((1, LANE - part), scale.dtype)
    out_copy.wait()
    for s in range(0, sections, 2):
        product = jnp.dot(
            hidden,
            jnp.concatenate([held[s, units:, :], held[s + 1, units:, :]], axis=1),
            preferred_element_type=jnp.float32,
        )
        columns = [scale[:, (s + i) * part : (s + i + 1) * part] for i in range(2)]
        product = product * jnp.concatenate([columns[0], edge, columns[1], edge], axis=1)
        product = product.astype(jnp.bfloat16)
        for i in range(2):
            o_ref[:, (s + i) * part : (s + i + 1) * part] = product[:, i * LANE : i * LANE + part]


def sum_body(x_ref, rows_ref, o_ref):
    blocks = rows_ref.shape[0]
    for b in range(blocks):
        branch = x_ref[0, b].astype(jnp.float32)
        for t in range(1, x_ref.shape[0]):
            branch += x_ref[t, b].astype(jnp.float32)
        values = rows_ref[b].astype(jnp.float32)
        o_ref[b] = (values + branch).astype(o_ref.dtype)


def local(sections, groups, patches, plan, norm_gain, proj_in, proj_out, layer_scale):
    blocks, rows, width = patches.shape
    bf16 = jnp.bfloat16
    part, units = proj_in.shape
    shape = jax.ShapeDtypeStruct((sections * blocks, rows, LANE), bf16)
    weights, tiles = call(
        first_body,
        (jax.ShapeDtypeStruct((2 * units, LANE), bf16), shape),
        [VMEM, VMEM, VMEM],
        n_out=2,
        limit=60,
    )(patches, proj_in.T, proj_out)
    weights = lax.all_gather(weights, "section", axis=0, tiled=False)
    tiles = lax.all_to_all(tiles, "section", 0, 0, tiled=True)
    tiles = call(order_body, shape, [SMEM, VMEM], limit=60)(plan, tiles)
    tiles = lax.all_to_all(tiles, "section", 0, 0, tiled=True)
    own, copies = call(
        norm_body,
        (
            jax.ShapeDtypeStruct((blocks, rows, width), bf16),
            jax.ShapeDtypeStruct((groups, blocks, rows, width), bf16),
        ),
        [VMEM, VMEM],
        n_out=2,
    )(tiles, norm_gain)

    all_rows = groups * blocks * rows
    normed = lax.all_to_all(copies.reshape(all_rows, width), "tensor", 0, 0, tiled=True)
    partial_sum = call(
        functools.partial(mlp_body, part),
        jax.ShapeDtypeStruct((all_rows, width), bf16),
        [ANY, ANY, VMEM],
        flops=4 * all_rows * width * units,
        moved=10 * 1024 * 1024,
        scratch=[
            pltpu.VMEM((all_rows, width), bf16),
            pltpu.VMEM((all_rows, sections * LANE), bf16),
            pltpu.VMEM((sections, 2 * units, LANE), bf16),
            pltpu.SemaphoreType.DMA(()),
            pltpu.SemaphoreType.DMA(()),
            pltpu.SemaphoreType.DMA(()),
        ],
        limit=60,
    )(normed, weights, layer_scale)
    terms = lax.all_to_all(partial_sum, "tensor", 0, 0, tiled=True)
    return call(
        sum_body,
        jax.ShapeDtypeStruct((blocks, rows, width), bf16),
        [VMEM, VMEM],
    )(terms.reshape(groups, blocks, rows, width), own)


def solution(mesh):
    return jax.shard_map(
        functools.partial(local, mesh.shape["section"], mesh.shape["tensor"]),
        mesh=mesh,
        in_specs=(
            P("section", "tensor", None),
            P(),
            P(),
            P("section", "tensor"),
            P("tensor", "section"),
            P(),
        ),
        out_specs=P("section", "tensor", None),
        check_vma=False,
    )
```

```python
import functools

import jax
import jax.numpy as jnp
from jax import lax
from jax.experimental import pallas as pl
from jax.experimental.pallas import tpu as pltpu
from jax.sharding import PartitionSpec as P

LANE = 128
VMEM = pl.BlockSpec(memory_space=pltpu.VMEM)
ANY = pl.BlockSpec(memory_space=pl.ANY)
SMEM = pl.BlockSpec(memory_space=pltpu.SMEM)


def call(body, out_shape, in_specs, flops=0, moved=0, n_out=1, scratch=(), limit=32):
    return pl.pallas_call(
        body,
        out_shape=out_shape,
        in_specs=in_specs,
        out_specs=VMEM if n_out == 1 else [VMEM] * n_out,
        scratch_shapes=list(scratch),
        compiler_params=pltpu.CompilerParams(vmem_limit_bytes=limit * 1024 * 1024),
        cost_estimate=pl.CostEstimate(flops=flops, bytes_accessed=moved, transcendentals=0),
    )


def first_body(x_ref, in_ref, out_ref, weights_ref, tiles_ref):
    part = in_ref.shape[1]
    kept = weights_ref.shape[0] // 2
    fold, chunk = kept // 4, part // 4
    for k, ref in enumerate((in_ref, out_ref)):
        at = k * kept
        weights_ref[at : at + kept, :part] = ref[:kept, :]
        for j in range(4):
            weights_ref[at + j * fold : at + (j + 1) * fold, part : part + chunk] = ref[
                kept:, j * chunk : (j + 1) * chunk
            ]
        edge = LANE - part - chunk
        weights_ref[at : at + kept, part + chunk :] = jnp.zeros((kept, edge), weights_ref.dtype)
    blocks, rows, width = x_ref.shape
    for m in range(tiles_ref.shape[0] // blocks):
        for b in range(blocks):
            if (m + 1) * LANE <= width:
                tiles_ref[m * blocks + b] = x_ref[b, :, m * LANE : (m + 1) * LANE]
            else:
                tiles_ref[m * blocks + b] = jnp.zeros((rows, LANE), tiles_ref.dtype)


def order_body(plan_ref, x_ref, _, o_ref):
    for p in range(o_ref.shape[0]):
        o_ref[p] = x_ref[plan_ref[p]]


def norm_body(x_ref, gain_ref, _, rows_ref, copies_ref):
    blocks, rows, width = rows_ref.shape
    tiles = width // LANE
    for b in range(blocks):
        whole = jnp.concatenate([x_ref[m * blocks + b] for m in range(tiles)], axis=-1)
        rows_ref[b] = whole
        values = whole.astype(jnp.float32)
        mean_square = jnp.sum(values * values, axis=-1, keepdims=True) * (1.0 / width)
        normed = values * lax.rsqrt(mean_square + 1e-06) * gain_ref[...].reshape(1, width)
        normed = normed.astype(jnp.bfloat16)
        for t in range(copies_ref.shape[0]):
            copies_ref[t, b] = normed


def pair_body(mine_ref, other_ref, o_ref):
    core = lax.rem(lax.axis_index("section"), 2)
    o_ref[core] = mine_ref[...]
    o_ref[1 - core] = other_ref[...]


def opened(ref, index, at, kept, part):
    fold, chunk = kept // 4, part // 4
    rest = [ref[index, at + j * fold : at + (j + 1) * fold, part : part + chunk] for j in range(4)]
    rest.append(jnp.zeros((fold, LANE - part), ref.dtype))
    return jnp.concatenate([ref[index, at : at + kept, :], jnp.concatenate(rest, axis=1)], axis=0)


def mlp_body(part, units, plan, x_ref, scale_ref, *refs):
    shard_refs = refs[:-4]
    o_ref, spread, scales, results = refs[-4:]
    chips, rows, _ = spread.shape
    kept = units * 4 // 5
    me = lax.axis_index("section")
    core = lax.rem(me, 2)
    here = lax.div(me, 2)
    blank = jnp.zeros((rows, LANE - part), x_ref.dtype)
    edge = jnp.zeros((1, LANE - part), scale_ref.dtype)
    scale = scale_ref[...].reshape(1, 2 * chips * part)
    for c in range(chips):
        tiles, factors = [], []
        for s in (2 * c, 2 * c + 1):
            tiles += [x_ref[:, s * part : (s + 1) * part], blank]
            factors += [scale[:, s * part : (s + 1) * part], edge]
        spread[c] = jnp.concatenate(tiles, axis=1)
        scales[c] = jnp.concatenate(factors, axis=1)
    places = [
        lax.rem(here + away * (1 - 2 * core) + 2 * chips, chips) for _, _, away in plan
    ]
    total = jnp.zeros((rows, units), jnp.float32)
    for (r, i, _), place in zip(plan, places):
        pair = [opened(shard_refs[r], 2 * i + k, 0, kept, part) for k in range(2)]
        total += lax.dot_general(
            spread[place],
            jnp.concatenate(pair, axis=1),
            (((1,), (1,)), ((), ())),
            preferred_element_type=jnp.float32,
        )
    hidden = 0.5 * total * (1.0 + lax.erf(total * (0.5**0.5)))
    hidden = hidden.astype(jnp.bfloat16)
    for (r, i, _), place in zip(plan, places):
        pair = [opened(shard_refs[r], 2 * i + k, kept, kept, part) for k in range(2)]
        product = jnp.dot(
            hidden, jnp.concatenate(pair, axis=1), preferred_element_type=jnp.float32
        )
        results[place] = (product * scales[place]).astype(jnp.bfloat16)
    for s in range(2 * chips):
        at = (s % 2) * LANE
        o_ref[:, s * part : (s + 1) * part] = results[s // 2, :, at : at + part]


def gather_weights(mine, sections):
    chips = sections // 2
    half = chips // 2
    swap = [(i, i ^ 1) for i in range(sections)]
    step = [(i, (i + (2 if i % 2 == 0 else -2)) % sections) for i in range(sections)]
    other = lax.ppermute(mine, "section", swap)
    now = call(pair_body, jax.ShapeDtypeStruct((2,) + mine.shape, mine.dtype), [VMEM, VMEM])(
        mine, other
    )
    arrays, plan, waiting = [now], [(0, 0, 0)], []
    for k in range(1, half + 1):
        now = lax.ppermute(now, "section", step)
        plan.append((len(arrays), 0, -k))
        arrays.append(now)
        if k < half:
            waiting.append((k, now))
        if k in (half // 2 - 1, half - 2, half - 1):
            group = [w for _, w in waiting]
            group = group[0] if len(group) == 1 else jnp.concatenate(group, axis=0)
            for i, (away, _) in enumerate(waiting):
                plan.append((len(arrays), i, away))
            arrays.append(lax.ppermute(group, "section", swap))
            waiting = []
    return arrays, plan


def sum_body(x_ref, rows_ref, o_ref):
    blocks = rows_ref.shape[0]
    for b in range(blocks):
        branch = x_ref[0, b].astype(jnp.float32)
        for t in range(1, x_ref.shape[0]):
            branch += x_ref[t, b].astype(jnp.float32)
        values = rows_ref[b].astype(jnp.float32)
        o_ref[b] = (values + branch).astype(o_ref.dtype)


def local(sections, groups, patches, plan, norm_gain, proj_in, proj_out, layer_scale):
    blocks, rows, width = patches.shape
    bf16 = jnp.bfloat16
    part, units = proj_in.shape
    shape = jax.ShapeDtypeStruct((sections * blocks, rows, LANE), bf16)
    weights, tiles = call(
        first_body,
        (jax.ShapeDtypeStruct((2 * (units * 4 // 5), LANE), bf16), shape),
        [VMEM, VMEM, VMEM],
        n_out=2,
        limit=60,
    )(patches, proj_in.T, proj_out)
    shards, where = gather_weights(weights, sections)
    steps = [shards[r] for r, i, away in where if away <= 0]
    tiles = lax.all_to_all(tiles, "section", 0, 0, tiled=True)
    tiles = call(order_body, shape, [SMEM, VMEM, ANY], limit=60)(plan, tiles, steps[2])
    tiles = lax.all_to_all(tiles, "section", 0, 0, tiled=True)
    own, copies = call(
        norm_body,
        (
            jax.ShapeDtypeStruct((blocks, rows, width), bf16),
            jax.ShapeDtypeStruct((groups, blocks, rows, width), bf16),
        ),
        [VMEM, VMEM, ANY],
        n_out=2,
    )(tiles, norm_gain, steps[min(5, len(steps) - 1)])

    all_rows = groups * blocks * rows
    normed = lax.all_to_all(copies.reshape(all_rows, width), "tensor", 0, 0, tiled=True)
    partial_sum = call(
        functools.partial(mlp_body, part, units, where),
        jax.ShapeDtypeStruct((all_rows, width), bf16),
        [VMEM] * (2 + len(shards)),
        flops=4 * all_rows * width * units,
        moved=10 * 1024 * 1024,
        scratch=[
            pltpu.VMEM((sections // 2, all_rows, 2 * LANE), bf16),
            pltpu.VMEM((sections // 2, 1, 2 * LANE), jnp.float32),
            pltpu.VMEM((sections // 2, all_rows, 2 * LANE), bf16),
        ],
        limit=60,
    )(normed, layer_scale, *shards)
    terms = lax.all_to_all(partial_sum, "tensor", 0, 0, tiled=True)
    return call(
        sum_body,
        jax.ShapeDtypeStruct((blocks, rows, width), bf16),
        [VMEM, VMEM],
    )(terms.reshape(groups, blocks, rows, width), own)


def solution(mesh):
    return jax.shard_map(
        functools.partial(local, mesh.shape["section"], mesh.shape["tensor"]),
        mesh=mesh,
        in_specs=(
            P("section", "tensor", None),
            P(),
            P(),
            P("section", "tensor"),
            P("tensor", "section"),
            P(),
        ),
        out_specs=P("section", "tensor", None),
        check_vma=False,
    )
```

```python
import functools

import jax
import jax.numpy as jnp
from jax import lax
from jax.experimental import pallas as pl
from jax.experimental.pallas import tpu as pltpu
from jax.sharding import PartitionSpec as P

LANE = 128
VMEM = pl.BlockSpec(memory_space=pltpu.VMEM)
ANY = pl.BlockSpec(memory_space=pl.ANY)
SMEM = pl.BlockSpec(memory_space=pltpu.SMEM)


def call(body, out_shape, in_specs, flops=0, moved=0, n_out=1, scratch=(), limit=32, out=VMEM):
    return pl.pallas_call(
        body,
        out_shape=out_shape,
        in_specs=in_specs,
        out_specs=out if n_out == 1 else [out] * n_out,
        scratch_shapes=list(scratch),
        compiler_params=pltpu.CompilerParams(vmem_limit_bytes=limit * 1024 * 1024),
        cost_estimate=pl.CostEstimate(flops=flops, bytes_accessed=moved, transcendentals=0),
    )


def first_body(x_ref, in_ref, out_ref, gain_ref, scale_ref, weights_ref, tiles_ref, both_ref):
    both_ref[0] = gain_ref[...]
    both_ref[1] = scale_ref[...]
    part = in_ref.shape[1]
    kept = weights_ref.shape[0] // 2
    fold, chunk = kept // 4, part // 4
    for k, ref in enumerate((in_ref, out_ref)):
        at = k * kept
        weights_ref[at : at + kept, :part] = ref[:kept, :]
        for j in range(4):
            weights_ref[at + j * fold : at + (j + 1) * fold, part : part + chunk] = ref[
                kept:, j * chunk : (j + 1) * chunk
            ]
        edge = LANE - part - chunk
        weights_ref[at : at + kept, part + chunk :] = jnp.zeros((kept, edge), weights_ref.dtype)
    blocks, rows, width = x_ref.shape
    for m in range(tiles_ref.shape[0] // blocks):
        for b in range(blocks):
            if (m + 1) * LANE <= width:
                tiles_ref[m * blocks + b] = x_ref[b, :, m * LANE : (m + 1) * LANE]
            else:
                tiles_ref[m * blocks + b] = jnp.zeros((rows, LANE), tiles_ref.dtype)


def order_body(plan_ref, x_ref, o_ref):
    for p in range(o_ref.shape[0]):
        o_ref[p] = x_ref[plan_ref[p]]


def norm_body(x_ref, both_ref, rows_ref, copies_ref, scale_out_ref):
    blocks, rows, width = rows_ref.shape
    tiles = width // LANE
    for b in range(blocks):
        whole = jnp.concatenate([x_ref[m * blocks + b] for m in range(tiles)], axis=-1)
        rows_ref[b] = whole
        values = whole.astype(jnp.float32)
        mean_square = jnp.sum(values * values, axis=-1, keepdims=True) * (1.0 / width)
        normed = values * lax.rsqrt(mean_square + 1e-06) * both_ref[:1, :]
        normed = normed.astype(jnp.bfloat16)
        for t in range(copies_ref.shape[0]):
            copies_ref[t, b] = normed
    scale_out_ref[...] = both_ref[1:, :]


def spread_body(part, x_ref, o_ref):
    blank = jnp.zeros((x_ref.shape[0], LANE - part), x_ref.dtype)
    for s in range(o_ref.shape[1] // LANE):
        o_ref[:, s * LANE : (s + 1) * LANE] = jnp.concatenate(
            [x_ref[:, s * part : (s + 1) * part], blank], axis=1
        )


def opened(ref, index, at, kept, part):
    fold, chunk = kept // 4, part // 4
    rest = [ref[index, at + j * fold : at + (j + 1) * fold, part : part + chunk] for j in range(4)]
    rest.append(jnp.zeros((fold, LANE - part), ref.dtype))
    return jnp.concatenate([ref[index, at : at + kept, :], jnp.concatenate(rest, axis=1)], axis=0)


def mlp_body(part, units, x_hbm, w_hbm, o_hbm, x_ref, held, o_ref, x_sem, in_sem, out_sem, o_sems):
    sections, both, _ = held.shape
    kept = both // 2
    rows = x_ref.shape[0]
    x_copy = pltpu.make_async_copy(x_hbm, x_ref, x_sem)
    x_copy.start()
    first, second = pl.ds(0, kept), pl.ds(kept, kept)
    in_copy = pltpu.make_async_copy(w_hbm.at[:, first], held.at[:, first], in_sem)
    in_copy.start()
    out_copy = pltpu.make_async_copy(w_hbm.at[:, second], held.at[:, second], out_sem)
    out_copy.start()
    x_copy.wait()
    in_copy.wait()
    total = jnp.zeros((rows, units), jnp.float32)
    for s in range(0, sections, 2):
        pair = [opened(held, s + k, 0, kept, part) for k in range(2)]
        total += lax.dot_general(
            x_ref[:, s * LANE : (s + 2) * LANE],
            jnp.concatenate(pair, axis=1),
            (((1,), (1,)), ((), ())),
            preferred_element_type=jnp.float32,
        )
    hidden = 0.5 * total * (1.0 + lax.erf(total * (0.5**0.5)))
    hidden = hidden.astype(jnp.bfloat16)
    out_copy.wait()
    pairs = [
        jnp.concatenate([opened(held, s + k, kept, kept, part) for k in range(2)], axis=1)
        for s in range(0, sections, 2)
    ]
    size = rows // 2
    copies = []
    for h in range(2):
        own = slice(h * size, (h + 1) * size)
        for j, pair in enumerate(pairs):
            product = jnp.dot(hidden[own], pair, preferred_element_type=jnp.float32)
            product = product.astype(jnp.bfloat16)
            for i in range(2):
                at = (2 * j + i) * part
                o_ref[own, at : at + part] = product[:, i * LANE : i * LANE + part]
        place = pl.ds(h * size, size)
        copy = pltpu.make_async_copy(o_ref.at[place], o_hbm.at[place], o_sems.at[h])
        copy.start()
        copies.append(copy)
    for copy in copies:
        copy.wait()


def sum_body(x_ref, rows_ref, scale_ref, o_ref):
    blocks = rows_ref.shape[0]
    for b in range(blocks):
        branch = x_ref[0, b].astype(jnp.float32)
        for t in range(1, x_ref.shape[0]):
            branch += x_ref[t, b].astype(jnp.float32)
        values = rows_ref[b].astype(jnp.float32)
        o_ref[b] = (values + scale_ref[...] * branch).astype(o_ref.dtype)


def local(sections, groups, patches, plan, norm_gain, proj_in, proj_out, layer_scale):
    blocks, rows, width = patches.shape
    bf16 = jnp.bfloat16
    part, units = proj_in.shape
    kept = units * 4 // 5
    shape = jax.ShapeDtypeStruct((sections * blocks, rows, LANE), bf16)
    weights, tiles, gain_and_scale = call(
        first_body,
        (
            jax.ShapeDtypeStruct((2 * kept, LANE), bf16),
            shape,
            jax.ShapeDtypeStruct((2, width), jnp.float32),
        ),
        [VMEM] * 5,
        n_out=3,
        limit=60,
    )(patches, proj_in.T, proj_out, norm_gain, layer_scale)
    weights = lax.all_gather(weights, "section", axis=0, tiled=False)
    tiles = lax.all_to_all(tiles, "section", 0, 0, tiled=True)
    tiles = call(order_body, shape, [SMEM, VMEM])(plan, tiles)
    tiles = lax.all_to_all(tiles, "section", 0, 0, tiled=True)
    own, copies, scale = call(
        norm_body,
        (
            jax.ShapeDtypeStruct((blocks, rows, width), bf16),
            jax.ShapeDtypeStruct((groups, blocks, rows, width), bf16),
            jax.ShapeDtypeStruct((1, width), jnp.float32),
        ),
        [VMEM, VMEM],
        n_out=3,
    )(tiles, gain_and_scale)

    all_rows = groups * blocks * rows
    normed = lax.all_to_all(copies.reshape(all_rows, width), "tensor", 0, 0, tiled=True)
    spread = call(
        functools.partial(spread_body, part),
        jax.ShapeDtypeStruct((all_rows, sections * LANE), bf16),
        [VMEM],
    )(normed)
    partial_sum = call(
        functools.partial(mlp_body, part, units),
        jax.ShapeDtypeStruct((all_rows, width), bf16),
        [ANY, ANY],
        flops=4 * all_rows * width * units,
        moved=10 * 1024 * 1024,
        scratch=[
            pltpu.VMEM((all_rows, sections * LANE), bf16),
            pltpu.VMEM((sections, 2 * kept, LANE), bf16),
            pltpu.VMEM((all_rows, width), bf16),
            pltpu.SemaphoreType.DMA(()),
            pltpu.SemaphoreType.DMA(()),
            pltpu.SemaphoreType.DMA(()),
            pltpu.SemaphoreType.DMA((2,)),
        ],
        limit=60,
        out=ANY,
    )(spread, weights)
    terms = lax.all_to_all(partial_sum, "tensor", 0, 0, tiled=True)
    return call(
        sum_body,
        jax.ShapeDtypeStruct((blocks, rows, width), bf16),
        [VMEM, VMEM, VMEM],
    )(terms.reshape(groups, blocks, rows, width), own, scale)


def solution(mesh):
    return jax.shard_map(
        functools.partial(local, mesh.shape["section"], mesh.shape["tensor"]),
        mesh=mesh,
        in_specs=(
            P("section", "tensor", None),
            P(),
            P(),
            P("section", "tensor"),
            P("tensor", "section"),
            P(),
        ),
        out_specs=P("section", "tensor", None),
        check_vma=False,
    )
```

```python
import functools

import jax
import jax.numpy as jnp
from jax import lax
from jax.experimental import pallas as pl
from jax.experimental.pallas import tpu as pltpu
from jax.sharding import PartitionSpec as P

LANE = 128
VMEM = pl.BlockSpec(memory_space=pltpu.VMEM)
ANY = pl.BlockSpec(memory_space=pl.ANY)
SMEM = pl.BlockSpec(memory_space=pltpu.SMEM)


def call(body, out_shape, in_specs, flops=0, moved=0, n_out=1, scratch=(), limit=32):
    return pl.pallas_call(
        body,
        out_shape=out_shape,
        in_specs=in_specs,
        out_specs=VMEM if n_out == 1 else [VMEM] * n_out,
        scratch_shapes=list(scratch),
        compiler_params=pltpu.CompilerParams(vmem_limit_bytes=limit * 1024 * 1024),
        cost_estimate=pl.CostEstimate(flops=flops, bytes_accessed=moved, transcendentals=0),
    )


def first_body(x_ref, in_ref, out_ref, gain_ref, scale_ref, weights_ref, tiles_ref, both_ref):
    both_ref[0] = gain_ref[...]
    both_ref[1] = scale_ref[...]
    part = in_ref.shape[1]
    kept = weights_ref.shape[0] // 2
    fold, chunk = kept // 4, part // 4
    for k, ref in enumerate((in_ref, out_ref)):
        at = k * kept
        weights_ref[at : at + kept, :part] = ref[:kept, :]
        for j in range(4):
            weights_ref[at + j * fold : at + (j + 1) * fold, part : part + chunk] = ref[
                kept:, j * chunk : (j + 1) * chunk
            ]
        edge = LANE - part - chunk
        weights_ref[at : at + kept, part + chunk :] = jnp.zeros((kept, edge), weights_ref.dtype)
    blocks, rows, width = x_ref.shape
    for m in range(tiles_ref.shape[0] // blocks):
        for b in range(blocks):
            if (m + 1) * LANE <= width:
                tiles_ref[m * blocks + b] = x_ref[b, :, m * LANE : (m + 1) * LANE]
            else:
                tiles_ref[m * blocks + b] = jnp.zeros((rows, LANE), tiles_ref.dtype)


def order_body(plan_ref, x_ref, o_ref):
    for p in range(o_ref.shape[0]):
        o_ref[p] = x_ref[plan_ref[p]]


def norm_body(x_ref, both_ref, rows_ref, copies_ref, scale_out_ref):
    blocks, rows, width = rows_ref.shape
    tiles = width // LANE
    for b in range(blocks):
        whole = jnp.concatenate([x_ref[m * blocks + b] for m in range(tiles)], axis=-1)
        rows_ref[b] = whole
        values = whole.astype(jnp.float32)
        mean_square = jnp.sum(values * values, axis=-1, keepdims=True) * (1.0 / width)
        normed = values * lax.rsqrt(mean_square + 1e-06) * both_ref[:1, :]
        normed = normed.astype(jnp.bfloat16)
        for t in range(copies_ref.shape[0]):
            copies_ref[t, b] = normed
    scale_out_ref[...] = both_ref[1:, :]


def opened(ref, index, at, kept, part):
    fold, chunk = kept // 4, part // 4
    rest = [ref[index, at + j * fold : at + (j + 1) * fold, part : part + chunk] for j in range(4)]
    rest.append(jnp.zeros((fold, LANE - part), ref.dtype))
    return jnp.concatenate([ref[index, at : at + kept, :], jnp.concatenate(rest, axis=1)], axis=0)


def mlp_body(part, units, x_ref, w_hbm, o_ref, spread, held, in_sem, out_sem):
    sections, both, _ = held.shape
    kept = both // 2
    first, second = pl.ds(0, kept), pl.ds(kept, kept)
    in_copy = pltpu.make_async_copy(w_hbm.at[:, first], held.at[:, first], in_sem)
    in_copy.start()
    out_copy = pltpu.make_async_copy(w_hbm.at[:, second], held.at[:, second], out_sem)
    out_copy.start()
    blank = jnp.zeros((x_ref.shape[0], LANE - part), x_ref.dtype)
    for s in range(sections):
        spread[:, s * LANE : (s + 1) * LANE] = jnp.concatenate(
            [x_ref[:, s * part : (s + 1) * part], blank], axis=1
        )
    in_copy.wait()
    total = jnp.zeros((x_ref.shape[0], units), jnp.float32)
    for s in range(0, sections, 2):
        pair = [opened(held, s + k, 0, kept, part) for k in range(2)]
        total += lax.dot_general(
            spread[:, s * LANE : (s + 2) * LANE],
            jnp.concatenate(pair, axis=1),
            (((1,), (1,)), ((), ())),
            preferred_element_type=jnp.float32,
        )
    hidden = 0.5 * total * (1.0 + lax.erf(total * (0.5**0.5)))
    hidden = hidden.astype(jnp.bfloat16)
    out_copy.wait()
    for s in range(0, sections, 2):
        pair = [opened(held, s + k, kept, kept, part) for k in range(2)]
        product = jnp.dot(
            hidden, jnp.concatenate(pair, axis=1), preferred_element_type=jnp.float32
        ).astype(jnp.bfloat16)
        for i in range(2):
            at = (s + i) * part
            o_ref[:, at : at + part] = product[:, i * LANE : i * LANE + part]


def sum_body(x_ref, rows_ref, scale_ref, o_ref):
    blocks = rows_ref.shape[0]
    for b in range(blocks):
        branch = x_ref[0, b].astype(jnp.float32)
        for t in range(1, x_ref.shape[0]):
            branch += x_ref[t, b].astype(jnp.float32)
        values = rows_ref[b].astype(jnp.float32)
        o_ref[b] = (values + scale_ref[...] * branch).astype(o_ref.dtype)


def local(sections, groups, patches, plan, norm_gain, proj_in, proj_out, layer_scale):
    blocks, rows, width = patches.shape
    bf16 = jnp.bfloat16
    part, units = proj_in.shape
    kept = units * 4 // 5
    shape = jax.ShapeDtypeStruct((sections * blocks, rows, LANE), bf16)
    weights, tiles, gain_and_scale = call(
        first_body,
        (
            jax.ShapeDtypeStruct((2 * kept, LANE), bf16),
            shape,
            jax.ShapeDtypeStruct((2, width), jnp.float32),
        ),
        [VMEM] * 5,
        n_out=3,
        limit=60,
    )(patches, proj_in.T, proj_out, norm_gain, layer_scale)
    weights = lax.all_gather(weights, "section", axis=0, tiled=False)
    tiles = lax.all_to_all(tiles, "section", 0, 0, tiled=True)
    tiles = call(order_body, shape, [SMEM, VMEM])(plan, tiles)
    tiles = lax.all_to_all(tiles, "section", 0, 0, tiled=True)
    own, copies, scale = call(
        norm_body,
        (
            jax.ShapeDtypeStruct((blocks, rows, width), bf16),
            jax.ShapeDtypeStruct((groups, blocks, rows, width), bf16),
            jax.ShapeDtypeStruct((1, width), jnp.float32),
        ),
        [VMEM, VMEM],
        n_out=3,
    )(tiles, gain_and_scale)

    all_rows = groups * blocks * rows
    normed = lax.all_to_all(copies.reshape(all_rows, width), "tensor", 0, 0, tiled=True)
    partial_sum = call(
        functools.partial(mlp_body, part, units),
        jax.ShapeDtypeStruct((all_rows, width), bf16),
        [VMEM, ANY],
        flops=4 * all_rows * width * units,
        moved=10 * 1024 * 1024,
        scratch=[
            pltpu.VMEM((all_rows, sections * LANE), bf16),
            pltpu.VMEM((sections, 2 * kept, LANE), bf16),
            pltpu.SemaphoreType.DMA(()),
            pltpu.SemaphoreType.DMA(()),
        ],
        limit=50,
    )(normed, weights)
    terms = lax.all_to_all(partial_sum, "tensor", 0, 0, tiled=True)
    return call(
        sum_body,
        jax.ShapeDtypeStruct((blocks, rows, width), bf16),
        [VMEM, VMEM, VMEM],
    )(terms.reshape(groups, blocks, rows, width), own, scale)


def solution(mesh):
    return jax.shard_map(
        functools.partial(local, mesh.shape["section"], mesh.shape["tensor"]),
        mesh=mesh,
        in_specs=(
            P("section", "tensor", None),
            P(),
            P(),
            P("section", "tensor"),
            P("tensor", "section"),
            P(),
        ),
        out_specs=P("section", "tensor", None),
        check_vma=False,
    )
```

```python
import functools
import math

import jax
import jax.numpy as jnp
from jax import lax
from jax.experimental import pallas as pl
from jax.experimental.pallas import tpu as pltpu
from jax.sharding import Mesh, PartitionSpec as P

LANE = 128
VMEM = pl.BlockSpec(memory_space=pltpu.VMEM)
ANY = pl.BlockSpec(memory_space=pl.ANY)
SMEM = pl.BlockSpec(memory_space=pltpu.SMEM)


def call(body, out_shape, in_specs, flops=0, moved=0, n_out=1, scratch=(), limit=32):
    return pl.pallas_call(
        body,
        out_shape=out_shape,
        in_specs=in_specs,
        out_specs=VMEM if n_out == 1 else [VMEM] * n_out,
        scratch_shapes=list(scratch),
        compiler_params=pltpu.CompilerParams(vmem_limit_bytes=limit * 1024 * 1024),
        cost_estimate=pl.CostEstimate(flops=flops, bytes_accessed=moved, transcendentals=0),
    )


def first_body(x_ref, in_ref, out_ref, gain_ref, scale_ref, weights_ref, tiles_ref, both_ref):
    both_ref[0] = gain_ref[...]
    both_ref[1] = scale_ref[...]
    part = in_ref.shape[1]
    kept = weights_ref.shape[0] // 2
    fold, chunk = kept // 4, part // 4
    for k, ref in enumerate((in_ref, out_ref)):
        at = k * kept
        weights_ref[at : at + kept, :part] = ref[:kept, :]
        for j in range(4):
            weights_ref[at + j * fold : at + (j + 1) * fold, part : part + chunk] = ref[
                kept:, j * chunk : (j + 1) * chunk
            ]
        edge = LANE - part - chunk
        weights_ref[at : at + kept, part + chunk :] = jnp.zeros((kept, edge), weights_ref.dtype)
    blocks, rows, width = x_ref.shape
    for m in range(tiles_ref.shape[0] // blocks):
        for b in range(blocks):
            if (m + 1) * LANE <= width:
                tiles_ref[m * blocks + b] = x_ref[b, :, m * LANE : (m + 1) * LANE]
            else:
                tiles_ref[m * blocks + b] = jnp.zeros((rows, LANE), tiles_ref.dtype)


def order_body(plan_ref, x_ref, o_ref):
    for p in range(o_ref.shape[0]):
        o_ref[p] = x_ref[plan_ref[p]]


def norm_body(x_ref, both_ref, rows_ref, normed_ref, scale_out_ref):
    blocks, rows, width = rows_ref.shape
    tiles = width // LANE
    for b in range(blocks):
        whole = jnp.concatenate([x_ref[m * blocks + b] for m in range(tiles)], axis=-1)
        rows_ref[b] = whole
        values = whole.astype(jnp.float32)
        mean_square = jnp.sum(values * values, axis=-1, keepdims=True) * (1.0 / width)
        normed = values * lax.rsqrt(mean_square + 1e-06) * both_ref[:1, :]
        normed_ref[b] = normed.astype(jnp.bfloat16)
    scale_out_ref[...] = both_ref[1:, :]


def copies_body(x_ref, o_ref):
    for k in range(o_ref.shape[0]):
        o_ref[k] = x_ref[...]


def opened(ref, index, at, kept, part):
    fold, chunk = kept // 4, part // 4
    rest = [ref[index, at + j * fold : at + (j + 1) * fold, part : part + chunk] for j in range(4)]
    rest.append(jnp.zeros((fold, LANE - part), ref.dtype))
    return jnp.concatenate([ref[index, at : at + kept, :], jnp.concatenate(rest, axis=1)], axis=0)


def mlp_body(part, units, x_ref, w_hbm, o_ref, spread, held, in_sem, out_sem):
    sections, both, _ = held.shape
    kept = both // 2
    first, second = pl.ds(0, kept), pl.ds(kept, kept)
    in_copy = pltpu.make_async_copy(w_hbm.at[:, first], held.at[:, first], in_sem)
    in_copy.start()
    out_copy = pltpu.make_async_copy(w_hbm.at[:, second], held.at[:, second], out_sem)
    out_copy.start()
    blank = jnp.zeros((x_ref.shape[0], LANE - part), x_ref.dtype)
    for s in range(sections):
        spread[:, s * LANE : (s + 1) * LANE] = jnp.concatenate(
            [x_ref[:, s * part : (s + 1) * part], blank], axis=1
        )
    in_copy.wait()
    total = jnp.zeros((x_ref.shape[0], units), jnp.float32)
    for s in range(0, sections, 2):
        pair = [opened(held, s + k, 0, kept, part) for k in range(2)]
        total += lax.dot_general(
            spread[:, s * LANE : (s + 2) * LANE],
            jnp.concatenate(pair, axis=1),
            (((1,), (1,)), ((), ())),
            preferred_element_type=jnp.float32,
        )
    hidden = 0.5 * total * (1.0 + lax.erf(total * (0.5**0.5)))
    hidden = hidden.astype(jnp.bfloat16)
    out_copy.wait()
    for s in range(0, sections, 2):
        pair = [opened(held, s + k, kept, kept, part) for k in range(2)]
        product = jnp.dot(
            hidden, jnp.concatenate(pair, axis=1), preferred_element_type=jnp.float32
        ).astype(jnp.bfloat16)
        for i in range(2):
            at = (s + i) * part
            o_ref[:, at : at + part] = product[:, i * LANE : i * LANE + part]


def sum_body(x_ref, rows_ref, scale_ref, o_ref):
    blocks = rows_ref.shape[0]
    for b in range(blocks):
        branch = x_ref[0, b].astype(jnp.float32)
        for t in range(1, x_ref.shape[0]):
            branch += x_ref[t, b].astype(jnp.float32)
        values = rows_ref[b].astype(jnp.float32)
        o_ref[b] = (values + scale_ref[...] * branch).astype(o_ref.dtype)


def local(sections, groups, patches, plan, norm_gain, proj_in, proj_out, layer_scale):
    blocks, rows, width = patches.shape
    bf16 = jnp.bfloat16
    part, units = proj_in.shape
    kept = units * 4 // 5
    shape = jax.ShapeDtypeStruct((sections * blocks, rows, LANE), bf16)
    weights, tiles, gain_and_scale = call(
        first_body,
        (
            jax.ShapeDtypeStruct((2 * kept, LANE), bf16),
            shape,
            jax.ShapeDtypeStruct((2, width), jnp.float32),
        ),
        [VMEM] * 5,
        n_out=3,
        limit=60,
    )(patches, proj_in.T, proj_out, norm_gain, layer_scale)
    weights = lax.all_gather(weights, "section", axis=0, tiled=False)
    tiles = lax.all_to_all(tiles, "section", 0, 0, tiled=True)
    tiles = call(order_body, shape, [SMEM, VMEM])(plan, tiles)
    tiles = lax.all_to_all(tiles, "section", 0, 0, tiled=True)
    own, normed, scale = call(
        norm_body,
        (
            jax.ShapeDtypeStruct((blocks, rows, width), bf16),
            jax.ShapeDtypeStruct((blocks, rows, width), bf16),
            jax.ShapeDtypeStruct((1, width), jnp.float32),
        ),
        [VMEM, VMEM],
        n_out=3,
    )(tiles, gain_and_scale)

    all_rows = groups * blocks * rows
    normed = lax.all_gather(normed.reshape(blocks * rows, width), "x", axis=0, tiled=True)
    column = normed.shape[0]
    copies = jax.ShapeDtypeStruct((all_rows // column, column, width), bf16)
    normed = call(copies_body, copies, [VMEM])(normed)
    normed = lax.all_to_all(normed.reshape(all_rows, width), "y", 0, 0, tiled=True)
    partial_sum = call(
        functools.partial(mlp_body, part, units),
        jax.ShapeDtypeStruct((all_rows, width), bf16),
        [VMEM, ANY],
        flops=4 * all_rows * width * units,
        moved=10 * 1024 * 1024,
        scratch=[
            pltpu.VMEM((all_rows, sections * LANE), bf16),
            pltpu.VMEM((sections, 2 * kept, LANE), bf16),
            pltpu.SemaphoreType.DMA(()),
            pltpu.SemaphoreType.DMA(()),
        ],
        limit=50,
    )(normed, weights)
    terms = lax.all_to_all(partial_sum, ("y", "x"), 0, 0, tiled=True)
    return call(
        sum_body,
        jax.ShapeDtypeStruct((blocks, rows, width), bf16),
        [VMEM, VMEM, VMEM],
    )(terms.reshape(groups, blocks, rows, width), own, scale)


def solution(mesh):
    sections, groups = mesh.shape["section"], mesh.shape["tensor"]
    side = math.isqrt(groups)
    plane = Mesh(mesh.devices.reshape(sections, groups // side, side), ("section", "x", "y"))
    tensor = ("x", "y")
    return jax.shard_map(
        functools.partial(local, sections, groups),
        mesh=plane,
        in_specs=(
            P("section", tensor, None),
            P(),
            P(),
            P("section", tensor),
            P(tensor, "section"),
            P(),
        ),
        out_specs=P("section", tensor, None),
        check_vma=False,
    )
```

```python
import functools
import math

import jax
import jax.numpy as jnp
from jax import lax
from jax.experimental import pallas as pl
from jax.experimental.pallas import tpu as pltpu
from jax.sharding import Mesh, PartitionSpec as P

LANE = 128
VMEM = pl.BlockSpec(memory_space=pltpu.VMEM)
ANY = pl.BlockSpec(memory_space=pl.ANY)
SMEM = pl.BlockSpec(memory_space=pltpu.SMEM)


def call(body, out_shape, in_specs, flops=0, moved=0, n_out=1, scratch=(), limit=32):
    return pl.pallas_call(
        body,
        out_shape=out_shape,
        in_specs=in_specs,
        out_specs=VMEM if n_out == 1 else [VMEM] * n_out,
        scratch_shapes=list(scratch),
        compiler_params=pltpu.CompilerParams(vmem_limit_bytes=limit * 1024 * 1024),
        cost_estimate=pl.CostEstimate(flops=flops, bytes_accessed=moved, transcendentals=0),
    )


def first_body(x_ref, in_ref, out_ref, gain_ref, scale_ref, weights_ref, tiles_ref, both_ref):
    both_ref[0] = gain_ref[...]
    both_ref[1] = scale_ref[...]
    part = in_ref.shape[1]
    kept = weights_ref.shape[0] // 2
    fold, chunk = kept // 4, part // 4
    for k, ref in enumerate((in_ref, out_ref)):
        at = k * kept
        weights_ref[at : at + kept, :part] = ref[:kept, :]
        for j in range(4):
            weights_ref[at + j * fold : at + (j + 1) * fold, part : part + chunk] = ref[
                kept:, j * chunk : (j + 1) * chunk
            ]
        edge = LANE - part - chunk
        weights_ref[at : at + kept, part + chunk :] = jnp.zeros((kept, edge), weights_ref.dtype)
    blocks, rows, width = x_ref.shape
    for m in range(tiles_ref.shape[0] // blocks):
        for b in range(blocks):
            if (m + 1) * LANE <= width:
                tiles_ref[m * blocks + b] = x_ref[b, :, m * LANE : (m + 1) * LANE]
            else:
                tiles_ref[m * blocks + b] = jnp.zeros((rows, LANE), tiles_ref.dtype)


def order_body(plan_ref, x_ref, o_ref):
    for p in range(o_ref.shape[0]):
        o_ref[p] = x_ref[plan_ref[p]]


def norm_body(x_ref, both_ref, rows_ref, copies_ref, scale_out_ref):
    blocks, rows, width = rows_ref.shape
    tiles = width // LANE
    for b in range(blocks):
        whole = jnp.concatenate([x_ref[m * blocks + b] for m in range(tiles)], axis=-1)
        rows_ref[b] = whole
        values = whole.astype(jnp.float32)
        mean_square = jnp.sum(values * values, axis=-1, keepdims=True) * (1.0 / width)
        normed = values * lax.rsqrt(mean_square + 1e-06) * both_ref[:1, :]
        normed = normed.astype(jnp.bfloat16)
        for t in range(copies_ref.shape[0]):
            copies_ref[t, b] = normed
    scale_out_ref[...] = both_ref[1:, :]


def opened(ref, index, at, kept, part):
    fold, chunk = kept // 4, part // 4
    rest = [ref[index, at + j * fold : at + (j + 1) * fold, part : part + chunk] for j in range(4)]
    rest.append(jnp.zeros((fold, LANE - part), ref.dtype))
    return jnp.concatenate([ref[index, at : at + kept, :], jnp.concatenate(rest, axis=1)], axis=0)


def mlp_body(part, units, x_ref, w_hbm, o_ref, spread, held, in_sem, out_sem):
    sections, both, _ = held.shape
    kept = both // 2
    first, second = pl.ds(0, kept), pl.ds(kept, kept)
    in_copy = pltpu.make_async_copy(w_hbm.at[:, first], held.at[:, first], in_sem)
    in_copy.start()
    out_copy = pltpu.make_async_copy(w_hbm.at[:, second], held.at[:, second], out_sem)
    out_copy.start()
    blank = jnp.zeros((x_ref.shape[0], LANE - part), x_ref.dtype)
    for s in range(sections):
        spread[:, s * LANE : (s + 1) * LANE] = jnp.concatenate(
            [x_ref[:, s * part : (s + 1) * part], blank], axis=1
        )
    in_copy.wait()
    total = jnp.zeros((x_ref.shape[0], units), jnp.float32)
    for s in range(0, sections, 2):
        pair = [opened(held, s + k, 0, kept, part) for k in range(2)]
        total += lax.dot_general(
            spread[:, s * LANE : (s + 2) * LANE],
            jnp.concatenate(pair, axis=1),
            (((1,), (1,)), ((), ())),
            preferred_element_type=jnp.float32,
        )
    hidden = 0.5 * total * (1.0 + lax.erf(total * (0.5**0.5)))
    hidden = hidden.astype(jnp.bfloat16)
    out_copy.wait()
    for s in range(0, sections, 2):
        pair = [opened(held, s + k, kept, kept, part) for k in range(2)]
        product = jnp.dot(
            hidden, jnp.concatenate(pair, axis=1), preferred_element_type=jnp.float32
        ).astype(jnp.bfloat16)
        for i in range(2):
            at = (s + i) * part
            o_ref[:, at : at + part] = product[:, i * LANE : i * LANE + part]


def sum_body(x_ref, rows_ref, scale_ref, o_ref):
    blocks = rows_ref.shape[0]
    for b in range(blocks):
        branch = x_ref[0, b].astype(jnp.float32)
        for t in range(1, x_ref.shape[0]):
            branch += x_ref[t, b].astype(jnp.float32)
        values = rows_ref[b].astype(jnp.float32)
        o_ref[b] = (values + scale_ref[...] * branch).astype(o_ref.dtype)


def local(sections, groups, patches, plan, norm_gain, proj_in, proj_out, layer_scale):
    blocks, rows, width = patches.shape
    bf16 = jnp.bfloat16
    part, units = proj_in.shape
    kept = units * 4 // 5
    shape = jax.ShapeDtypeStruct((sections * blocks, rows, LANE), bf16)
    weights, tiles, gain_and_scale = call(
        first_body,
        (
            jax.ShapeDtypeStruct((2 * kept, LANE), bf16),
            shape,
            jax.ShapeDtypeStruct((2, width), jnp.float32),
        ),
        [VMEM] * 5,
        n_out=3,
        limit=60,
    )(patches, proj_in.T, proj_out, norm_gain, layer_scale)
    weights = lax.all_gather(weights, "section", axis=0, tiled=False)
    tiles = lax.all_to_all(tiles, "section", 0, 0, tiled=True)
    tiles = call(order_body, shape, [SMEM, VMEM])(plan, tiles)
    tiles = lax.all_to_all(tiles, "section", 0, 0, tiled=True)
    own, copies, scale = call(
        norm_body,
        (
            jax.ShapeDtypeStruct((blocks, rows, width), bf16),
            jax.ShapeDtypeStruct((groups, blocks, rows, width), bf16),
            jax.ShapeDtypeStruct((1, width), jnp.float32),
        ),
        [VMEM, VMEM],
        n_out=3,
    )(tiles, gain_and_scale)

    all_rows = groups * blocks * rows
    normed = lax.all_to_all(copies.reshape(all_rows, width), ("y", "x"), 0, 0, tiled=True)
    partial_sum = call(
        functools.partial(mlp_body, part, units),
        jax.ShapeDtypeStruct((all_rows, width), bf16),
        [VMEM, ANY],
        flops=4 * all_rows * width * units,
        moved=10 * 1024 * 1024,
        scratch=[
            pltpu.VMEM((all_rows, sections * LANE), bf16),
            pltpu.VMEM((sections, 2 * kept, LANE), bf16),
            pltpu.SemaphoreType.DMA(()),
            pltpu.SemaphoreType.DMA(()),
        ],
        limit=50,
    )(normed, weights)
    terms = lax.all_to_all(partial_sum, ("y", "x"), 0, 0, tiled=True)
    return call(
        sum_body,
        jax.ShapeDtypeStruct((blocks, rows, width), bf16),
        [VMEM, VMEM, VMEM],
    )(terms.reshape(groups, blocks, rows, width), own, scale)


def solution(mesh):
    sections, groups = mesh.shape["section"], mesh.shape["tensor"]
    side = math.isqrt(groups)
    plane = Mesh(mesh.devices.reshape(sections, groups // side, side), ("section", "x", "y"))
    tensor = ("x", "y")
    return jax.shard_map(
        functools.partial(local, sections, groups),
        mesh=plane,
        in_specs=(
            P("section", tensor, None),
            P(),
            P(),
            P("section", tensor),
            P(tensor, "section"),
            P(),
        ),
        out_specs=P("section", tensor, None),
        check_vma=False,
    )
```

```python
import functools

import jax
import jax.numpy as jnp
from jax import lax
from jax.experimental import pallas as pl
from jax.experimental.pallas import tpu as pltpu
from jax.sharding import PartitionSpec as P

LANE = 128
VMEM = pl.BlockSpec(memory_space=pltpu.VMEM)
ANY = pl.BlockSpec(memory_space=pl.ANY)
SMEM = pl.BlockSpec(memory_space=pltpu.SMEM)


def call(body, out_shape, in_specs, flops=0, moved=0, n_out=1, scratch=(), limit=32):
    return pl.pallas_call(
        body,
        out_shape=out_shape,
        in_specs=in_specs,
        out_specs=VMEM if n_out == 1 else [VMEM] * n_out,
        scratch_shapes=list(scratch),
        compiler_params=pltpu.CompilerParams(vmem_limit_bytes=limit * 1024 * 1024),
        cost_estimate=pl.CostEstimate(flops=flops, bytes_accessed=moved, transcendentals=0),
    )


def first_body(x_ref, in_ref, out_ref, gain_ref, scale_ref, weights_ref, tiles_ref, both_ref):
    both_ref[0] = gain_ref[...]
    both_ref[1] = scale_ref[...]
    part = in_ref.shape[1]
    kept = weights_ref.shape[0] // 2
    fold, chunk = kept // 4, part // 4
    for k, ref in enumerate((in_ref, out_ref)):
        at = k * kept
        weights_ref[at : at + kept, :part] = ref[:kept, :]
        for j in range(4):
            weights_ref[at + j * fold : at + (j + 1) * fold, part : part + chunk] = ref[
                kept:, j * chunk : (j + 1) * chunk
            ]
        edge = LANE - part - chunk
        weights_ref[at : at + kept, part + chunk :] = jnp.zeros((kept, edge), weights_ref.dtype)
    blocks, rows, width = x_ref.shape
    for m in range(tiles_ref.shape[0] // blocks):
        for b in range(blocks):
            if (m + 1) * LANE <= width:
                tiles_ref[m * blocks + b] = x_ref[b, :, m * LANE : (m + 1) * LANE]
            else:
                tiles_ref[m * blocks + b] = jnp.zeros((rows, LANE), tiles_ref.dtype)


def order_body(plan_ref, x_ref, o_ref):
    for p in range(o_ref.shape[0]):
        o_ref[p] = x_ref[plan_ref[p]]


def norm_body(x_ref, both_ref, rows_ref, copies_ref, scale_out_ref):
    blocks, rows, width = rows_ref.shape
    tiles = width // LANE
    for b in range(blocks):
        whole = jnp.concatenate([x_ref[m * blocks + b] for m in range(tiles)], axis=-1)
        rows_ref[b] = whole
        values = whole.astype(jnp.float32)
        mean_square = jnp.sum(values * values, axis=-1, keepdims=True) * (1.0 / width)
        normed = values * lax.rsqrt(mean_square + 1e-06) * both_ref[:1, :]
        normed = normed.astype(jnp.bfloat16)
        for t in range(copies_ref.shape[0]):
            copies_ref[t, b] = normed
    scale_out_ref[...] = both_ref[1:, :]


def opened(ref, index, at, kept, part):
    fold, chunk = kept // 4, part // 4
    rest = [ref[index, at + j * fold : at + (j + 1) * fold, part : part + chunk] for j in range(4)]
    rest.append(jnp.zeros((fold, LANE - part), ref.dtype))
    return jnp.concatenate([ref[index, at : at + kept, :], jnp.concatenate(rest, axis=1)], axis=0)


def mlp_body(part, units, x_ref, w_hbm, o_ref, spread, held, in_sem, out_sem):
    sections, both, _ = held.shape
    kept = both // 2
    first, second = pl.ds(0, kept), pl.ds(kept, kept)
    in_copy = pltpu.make_async_copy(w_hbm.at[:, first], held.at[:, first], in_sem)
    in_copy.start()
    out_copy = pltpu.make_async_copy(w_hbm.at[:, second], held.at[:, second], out_sem)
    out_copy.start()
    blank = jnp.zeros((x_ref.shape[0], LANE - part), x_ref.dtype)
    for s in range(sections):
        spread[:, s * LANE : (s + 1) * LANE] = jnp.concatenate(
            [x_ref[:, s * part : (s + 1) * part], blank], axis=1
        )
    in_copy.wait()
    total = jnp.zeros((x_ref.shape[0], units), jnp.float32)
    for s in range(0, sections, 2):
        pair = [opened(held, s + k, 0, kept, part) for k in range(2)]
        total += lax.dot_general(
            spread[:, s * LANE : (s + 2) * LANE],
            jnp.concatenate(pair, axis=1),
            (((1,), (1,)), ((), ())),
            preferred_element_type=jnp.float32,
        )
    hidden = 0.5 * total * (1.0 + lax.erf(total * (0.5**0.5)))
    hidden = hidden.astype(jnp.bfloat16)
    out_copy.wait()
    for s in range(0, sections, 2):
        pair = [opened(held, s + k, kept, kept, part) for k in range(2)]
        product = jnp.dot(
            hidden, jnp.concatenate(pair, axis=1), preferred_element_type=jnp.float32
        ).astype(jnp.bfloat16)
        for i in range(2):
            at = (s + i) * part
            o_ref[:, at : at + part] = product[:, i * LANE : i * LANE + part]


def sum_body(x_ref, rows_ref, scale_ref, o_ref):
    blocks = rows_ref.shape[0]
    for b in range(blocks):
        branch = x_ref[0, b].astype(jnp.float32)
        for t in range(1, x_ref.shape[0]):
            branch += x_ref[t, b].astype(jnp.float32)
        values = rows_ref[b].astype(jnp.float32)
        o_ref[b] = (values + scale_ref[...] * branch).astype(o_ref.dtype)


def across_plane(x, sections, groups):
    order = list(range(groups))
    listed = [
        [section * groups + t for t in (order if section % 2 == 0 else order[::-1])]
        for section in range(sections)
    ]
    return lax.all_to_all(
        x, ("section", "tensor"), 0, 0, axis_index_groups=listed, tiled=True
    )


def local(sections, groups, patches, plan, norm_gain, proj_in, proj_out, layer_scale):
    blocks, rows, width = patches.shape
    bf16 = jnp.bfloat16
    part, units = proj_in.shape
    kept = units * 4 // 5
    shape = jax.ShapeDtypeStruct((sections * blocks, rows, LANE), bf16)
    weights, tiles, gain_and_scale = call(
        first_body,
        (
            jax.ShapeDtypeStruct((2 * kept, LANE), bf16),
            shape,
            jax.ShapeDtypeStruct((2, width), jnp.float32),
        ),
        [VMEM] * 5,
        n_out=3,
        limit=60,
    )(patches, proj_in.T, proj_out, norm_gain, layer_scale)
    weights = lax.all_gather(weights, "section", axis=0, tiled=False)
    tiles = lax.all_to_all(tiles, "section", 0, 0, tiled=True)
    tiles = call(order_body, shape, [SMEM, VMEM])(plan, tiles)
    tiles = lax.all_to_all(tiles, "section", 0, 0, tiled=True)
    own, copies, scale = call(
        norm_body,
        (
            jax.ShapeDtypeStruct((blocks, rows, width), bf16),
            jax.ShapeDtypeStruct((groups, blocks, rows, width), bf16),
            jax.ShapeDtypeStruct((1, width), jnp.float32),
        ),
        [VMEM, VMEM],
        n_out=3,
    )(tiles, gain_and_scale)

    all_rows = groups * blocks * rows
    normed = across_plane(copies.reshape(all_rows, width), sections, groups)
    partial_sum = call(
        functools.partial(mlp_body, part, units),
        jax.ShapeDtypeStruct((all_rows, width), bf16),
        [VMEM, ANY],
        flops=4 * all_rows * width * units,
        moved=10 * 1024 * 1024,
        scratch=[
            pltpu.VMEM((all_rows, sections * LANE), bf16),
            pltpu.VMEM((sections, 2 * kept, LANE), bf16),
            pltpu.SemaphoreType.DMA(()),
            pltpu.SemaphoreType.DMA(()),
        ],
        limit=50,
    )(normed, weights)
    terms = across_plane(partial_sum, sections, groups)
    return call(
        sum_body,
        jax.ShapeDtypeStruct((blocks, rows, width), bf16),
        [VMEM, VMEM, VMEM],
    )(terms.reshape(groups, blocks, rows, width), own, scale)


def solution(mesh):
    return jax.shard_map(
        functools.partial(local, mesh.shape["section"], mesh.shape["tensor"]),
        mesh=mesh,
        in_specs=(
            P("section", "tensor", None),
            P(),
            P(),
            P("section", "tensor"),
            P("tensor", "section"),
            P(),
        ),
        out_specs=P("section", "tensor", None),
        check_vma=False,
    )
```

```python
import functools

import jax
import jax.numpy as jnp
from jax import lax
from jax.experimental import pallas as pl
from jax.experimental.pallas import tpu as pltpu
from jax.sharding import PartitionSpec as P

LANE = 128
VMEM = pl.BlockSpec(memory_space=pltpu.VMEM)
ANY = pl.BlockSpec(memory_space=pl.ANY)
SMEM = pl.BlockSpec(memory_space=pltpu.SMEM)


def call(body, out_shape, in_specs, flops=0, moved=0, n_out=1, scratch=(), limit=32, out=VMEM):
    return pl.pallas_call(
        body,
        out_shape=out_shape,
        in_specs=in_specs,
        out_specs=out if n_out == 1 else [out] * n_out,
        scratch_shapes=list(scratch),
        compiler_params=pltpu.CompilerParams(vmem_limit_bytes=limit * 1024 * 1024),
        cost_estimate=pl.CostEstimate(flops=flops, bytes_accessed=moved, transcendentals=0),
    )


def first_body(x_ref, in_ref, out_ref, gain_ref, scale_ref, weights_ref, tiles_ref, both_ref):
    both_ref[0] = gain_ref[...]
    both_ref[1] = scale_ref[...]
    part = in_ref.shape[1]
    kept = weights_ref.shape[0] // 2
    fold, chunk = kept // 4, part // 4
    for k, ref in enumerate((in_ref, out_ref)):
        at = k * kept
        weights_ref[at : at + kept, :part] = ref[:kept, :]
        for j in range(4):
            weights_ref[at + j * fold : at + (j + 1) * fold, part : part + chunk] = ref[
                kept:, j * chunk : (j + 1) * chunk
            ]
        edge = LANE - part - chunk
        weights_ref[at : at + kept, part + chunk :] = jnp.zeros((kept, edge), weights_ref.dtype)
    blocks, rows, width = x_ref.shape
    for m in range(tiles_ref.shape[0] // blocks):
        for b in range(blocks):
            if (m + 1) * LANE <= width:
                tiles_ref[m * blocks + b] = x_ref[b, :, m * LANE : (m + 1) * LANE]
            else:
                tiles_ref[m * blocks + b] = jnp.zeros((rows, LANE), tiles_ref.dtype)


def order_body(plan_ref, x_ref, o_ref):
    for p in range(o_ref.shape[0]):
        o_ref[p] = x_ref[plan_ref[p]]


def norm_body(x_ref, both_ref, rows_ref, copies_ref, scale_out_ref):
    blocks, rows, width = rows_ref.shape
    tiles = width // LANE
    for b in range(blocks):
        whole = jnp.concatenate([x_ref[m * blocks + b] for m in range(tiles)], axis=-1)
        rows_ref[b] = whole
        values = whole.astype(jnp.float32)
        mean_square = jnp.sum(values * values, axis=-1, keepdims=True) * (1.0 / width)
        normed = values * lax.rsqrt(mean_square + 1e-06) * both_ref[:1, :]
        normed = normed.astype(jnp.bfloat16)
        for t in range(copies_ref.shape[0]):
            copies_ref[t, b] = normed
    scale_out_ref[...] = both_ref[1:, :]


def spread_body(part, x_ref, o_ref):
    blank = jnp.zeros((x_ref.shape[0], LANE - part), x_ref.dtype)
    for s in range(o_ref.shape[1] // LANE):
        o_ref[:, s * LANE : (s + 1) * LANE] = jnp.concatenate(
            [x_ref[:, s * part : (s + 1) * part], blank], axis=1
        )


def opened(ref, index, at, kept, part):
    fold, chunk = kept // 4, part // 4
    rest = [ref[index, at + j * fold : at + (j + 1) * fold, part : part + chunk] for j in range(4)]
    rest.append(jnp.zeros((fold, LANE - part), ref.dtype))
    return jnp.concatenate([ref[index, at : at + kept, :], jnp.concatenate(rest, axis=1)], axis=0)


def mlp_body(part, units, x_hbm, w_hbm, o_hbm, x_ref, held, o_ref, x_sem, in_sem, out_sem, o_sems):
    sections, both, _ = held.shape
    kept = both // 2
    rows = x_ref.shape[0]
    x_copy = pltpu.make_async_copy(x_hbm, x_ref, x_sem)
    x_copy.start()
    first, second = pl.ds(0, kept), pl.ds(kept, kept)
    in_copy = pltpu.make_async_copy(w_hbm.at[:, first], held.at[:, first], in_sem)
    in_copy.start()
    out_copy = pltpu.make_async_copy(w_hbm.at[:, second], held.at[:, second], out_sem)
    out_copy.start()
    x_copy.wait()
    in_copy.wait()
    total = jnp.zeros((rows, units), jnp.float32)
    for s in range(0, sections, 2):
        pair = [opened(held, s + k, 0, kept, part) for k in range(2)]
        total += lax.dot_general(
            x_ref[:, s * LANE : (s + 2) * LANE],
            jnp.concatenate(pair, axis=1),
            (((1,), (1,)), ((), ())),
            preferred_element_type=jnp.float32,
        )
    hidden = 0.5 * total * (1.0 + lax.erf(total * (0.5**0.5)))
    hidden = hidden.astype(jnp.bfloat16)
    out_copy.wait()
    pairs = [
        jnp.concatenate([opened(held, s + k, kept, kept, part) for k in range(2)], axis=1)
        for s in range(0, sections, 2)
    ]
    size = rows // 2
    copies = []
    for h in range(2):
        own = slice(h * size, (h + 1) * size)
        for j, pair in enumerate(pairs):
            product = jnp.dot(hidden[own], pair, preferred_element_type=jnp.float32)
            product = product.astype(jnp.bfloat16)
            for i in range(2):
                at = (2 * j + i) * part
                o_ref[own, at : at + part] = product[:, i * LANE : i * LANE + part]
        place = pl.ds(h * size, size)
        copy = pltpu.make_async_copy(o_ref.at[place], o_hbm.at[place], o_sems.at[h])
        copy.start()
        copies.append(copy)
    for copy in copies:
        copy.wait()


def sum_body(x_ref, rows_ref, scale_ref, o_ref):
    blocks = rows_ref.shape[0]
    for b in range(blocks):
        branch = x_ref[0, b].astype(jnp.float32)
        for t in range(1, x_ref.shape[0]):
            branch += x_ref[t, b].astype(jnp.float32)
        values = rows_ref[b].astype(jnp.float32)
        o_ref[b] = (values + scale_ref[...] * branch).astype(o_ref.dtype)


def across_plane(x, sections, groups):
    order = list(range(groups))
    listed = [
        [section * groups + t for t in (order if section % 2 == 0 else order[::-1])]
        for section in range(sections)
    ]
    return lax.all_to_all(
        x, ("section", "tensor"), 0, 0, axis_index_groups=listed, tiled=True
    )


def local(sections, groups, patches, plan, norm_gain, proj_in, proj_out, layer_scale):
    blocks, rows, width = patches.shape
    bf16 = jnp.bfloat16
    part, units = proj_in.shape
    kept = units * 4 // 5
    shape = jax.ShapeDtypeStruct((sections * blocks, rows, LANE), bf16)
    weights, tiles, gain_and_scale = call(
        first_body,
        (
            jax.ShapeDtypeStruct((2 * kept, LANE), bf16),
            shape,
            jax.ShapeDtypeStruct((2, width), jnp.float32),
        ),
        [VMEM] * 5,
        n_out=3,
        limit=60,
    )(patches, proj_in.T, proj_out, norm_gain, layer_scale)
    weights = lax.all_gather(weights, "section", axis=0, tiled=False)
    tiles = lax.all_to_all(tiles, "section", 0, 0, tiled=True)
    tiles = call(order_body, shape, [SMEM, VMEM])(plan, tiles)
    tiles = lax.all_to_all(tiles, "section", 0, 0, tiled=True)
    own, copies, scale = call(
        norm_body,
        (
            jax.ShapeDtypeStruct((blocks, rows, width), bf16),
            jax.ShapeDtypeStruct((groups, blocks, rows, width), bf16),
            jax.ShapeDtypeStruct((1, width), jnp.float32),
        ),
        [VMEM, VMEM],
        n_out=3,
    )(tiles, gain_and_scale)

    all_rows = groups * blocks * rows
    normed = across_plane(copies.reshape(all_rows, width), sections, groups)
    spread = call(
        functools.partial(spread_body, part),
        jax.ShapeDtypeStruct((all_rows, sections * LANE), bf16),
        [VMEM],
    )(normed)
    partial_sum = call(
        functools.partial(mlp_body, part, units),
        jax.ShapeDtypeStruct((all_rows, width), bf16),
        [ANY, ANY],
        flops=4 * all_rows * width * units,
        moved=10 * 1024 * 1024,
        scratch=[
            pltpu.VMEM((all_rows, sections * LANE), bf16),
            pltpu.VMEM((sections, 2 * kept, LANE), bf16),
            pltpu.VMEM((all_rows, width), bf16),
            pltpu.SemaphoreType.DMA(()),
            pltpu.SemaphoreType.DMA(()),
            pltpu.SemaphoreType.DMA(()),
            pltpu.SemaphoreType.DMA((2,)),
        ],
        limit=60,
        out=ANY,
    )(spread, weights)
    terms = across_plane(partial_sum, sections, groups)
    return call(
        sum_body,
        jax.ShapeDtypeStruct((blocks, rows, width), bf16),
        [VMEM, VMEM, VMEM],
    )(terms.reshape(groups, blocks, rows, width), own, scale)


def solution(mesh):
    return jax.shard_map(
        functools.partial(local, mesh.shape["section"], mesh.shape["tensor"]),
        mesh=mesh,
        in_specs=(
            P("section", "tensor", None),
            P(),
            P(),
            P("section", "tensor"),
            P("tensor", "section"),
            P(),
        ),
        out_specs=P("section", "tensor", None),
        check_vma=False,
    )
```

```python
import functools

import jax
import jax.numpy as jnp
from jax import lax
from jax.experimental import pallas as pl
from jax.experimental.pallas import tpu as pltpu
from jax.sharding import PartitionSpec as P

LANE = 128
VMEM = pl.BlockSpec(memory_space=pltpu.VMEM)
ANY = pl.BlockSpec(memory_space=pl.ANY)
SMEM = pl.BlockSpec(memory_space=pltpu.SMEM)


def call(body, out_shape, in_specs, flops=0, moved=0, n_out=1, scratch=(), limit=32):
    return pl.pallas_call(
        body,
        out_shape=out_shape,
        in_specs=in_specs,
        out_specs=VMEM if n_out == 1 else [VMEM] * n_out,
        scratch_shapes=list(scratch),
        compiler_params=pltpu.CompilerParams(vmem_limit_bytes=limit * 1024 * 1024),
        cost_estimate=pl.CostEstimate(flops=flops, bytes_accessed=moved, transcendentals=0),
    )


def first_body(x_ref, in_ref, out_ref, gain_ref, scale_ref, weights_ref, tiles_ref, both_ref):
    both_ref[0] = gain_ref[...]
    both_ref[1] = scale_ref[...]
    part = in_ref.shape[1]
    kept = weights_ref.shape[0] // 2
    fold, chunk = kept // 4, part // 4
    for k, ref in enumerate((in_ref, out_ref)):
        at = k * kept
        weights_ref[at : at + kept, :part] = ref[:kept, :]
        for j in range(4):
            weights_ref[at + j * fold : at + (j + 1) * fold, part : part + chunk] = ref[
                kept:, j * chunk : (j + 1) * chunk
            ]
        edge = LANE - part - chunk
        weights_ref[at : at + kept, part + chunk :] = jnp.zeros((kept, edge), weights_ref.dtype)
    blocks, rows, width = x_ref.shape
    for m in range(tiles_ref.shape[0] // blocks):
        for b in range(blocks):
            if (m + 1) * LANE <= width:
                tiles_ref[m * blocks + b] = x_ref[b, :, m * LANE : (m + 1) * LANE]
            else:
                tiles_ref[m * blocks + b] = jnp.zeros((rows, LANE), tiles_ref.dtype)


def order_body(plan_ref, x_ref, o_ref):
    for p in range(o_ref.shape[0]):
        o_ref[p] = x_ref[plan_ref[p]]


def norm_body(x_ref, both_ref, rows_ref, copies_ref, scale_out_ref):
    blocks, rows, width = rows_ref.shape
    tiles = width // LANE
    for b in range(blocks):
        whole = jnp.concatenate([x_ref[m * blocks + b] for m in range(tiles)], axis=-1)
        rows_ref[b] = whole
        values = whole.astype(jnp.float32)
        mean_square = jnp.sum(values * values, axis=-1, keepdims=True) * (1.0 / width)
        normed = values * lax.rsqrt(mean_square + 1e-06) * both_ref[:1, :]
        normed = normed.astype(jnp.bfloat16)
        for t in range(copies_ref.shape[0]):
            copies_ref[t, b] = normed
    scale_out_ref[...] = both_ref[1:, :]


def spread_body(part, x_ref, o_ref):
    blank = jnp.zeros((x_ref.shape[0], LANE - part), x_ref.dtype)
    for s in range(o_ref.shape[1] // LANE):
        o_ref[:, s * LANE : (s + 1) * LANE] = jnp.concatenate(
            [x_ref[:, s * part : (s + 1) * part], blank], axis=1
        )


def opened(ref, index, at, kept, part):
    fold, chunk = kept // 4, part // 4
    rest = [ref[index, at + j * fold : at + (j + 1) * fold, part : part + chunk] for j in range(4)]
    rest.append(jnp.zeros((fold, LANE - part), ref.dtype))
    return jnp.concatenate([ref[index, at : at + kept, :], jnp.concatenate(rest, axis=1)], axis=0)


def mlp_body(part, units, x_ref, w_hbm, o_ref, held, in_sem, out_sem):
    sections, both, _ = held.shape
    kept = both // 2
    first, second = pl.ds(0, kept), pl.ds(kept, kept)
    in_copy = pltpu.make_async_copy(w_hbm.at[:, first], held.at[:, first], in_sem)
    in_copy.start()
    out_copy = pltpu.make_async_copy(w_hbm.at[:, second], held.at[:, second], out_sem)
    out_copy.start()
    in_copy.wait()
    total = jnp.zeros((x_ref.shape[0], units), jnp.float32)
    for s in range(0, sections, 2):
        pair = [opened(held, s + k, 0, kept, part) for k in range(2)]
        total += lax.dot_general(
            x_ref[:, s * LANE : (s + 2) * LANE],
            jnp.concatenate(pair, axis=1),
            (((1,), (1,)), ((), ())),
            preferred_element_type=jnp.float32,
        )
    hidden = 0.5 * total * (1.0 + lax.erf(total * (0.5**0.5)))
    hidden = hidden.astype(jnp.bfloat16)
    out_copy.wait()
    for s in range(0, sections, 2):
        pair = [opened(held, s + k, kept, kept, part) for k in range(2)]
        product = jnp.dot(
            hidden, jnp.concatenate(pair, axis=1), preferred_element_type=jnp.float32
        ).astype(jnp.bfloat16)
        for i in range(2):
            at = (s + i) * part
            o_ref[:, at : at + part] = product[:, i * LANE : i * LANE + part]


def sum_body(x_ref, rows_ref, scale_ref, o_ref):
    blocks = rows_ref.shape[0]
    for b in range(blocks):
        branch = x_ref[0, b].astype(jnp.float32)
        for t in range(1, x_ref.shape[0]):
            branch += x_ref[t, b].astype(jnp.float32)
        values = rows_ref[b].astype(jnp.float32)
        o_ref[b] = (values + scale_ref[...] * branch).astype(o_ref.dtype)


def across_plane(x, sections, groups):
    order = list(range(groups))
    listed = [
        [section * groups + t for t in (order if section % 2 == 0 else order[::-1])]
        for section in range(sections)
    ]
    return lax.all_to_all(
        x, ("section", "tensor"), 0, 0, axis_index_groups=listed, tiled=True
    )


def local(sections, groups, patches, plan, norm_gain, proj_in, proj_out, layer_scale):
    blocks, rows, width = patches.shape
    bf16 = jnp.bfloat16
    part, units = proj_in.shape
    kept = units * 4 // 5
    shape = jax.ShapeDtypeStruct((sections * blocks, rows, LANE), bf16)
    weights, tiles, gain_and_scale = call(
        first_body,
        (
            jax.ShapeDtypeStruct((2 * kept, LANE), bf16),
            shape,
            jax.ShapeDtypeStruct((2, width), jnp.float32),
        ),
        [VMEM] * 5,
        n_out=3,
        limit=60,
    )(patches, proj_in.T, proj_out, norm_gain, layer_scale)
    weights = lax.all_gather(weights, "section", axis=0, tiled=False)
    tiles = lax.all_to_all(tiles, "section", 0, 0, tiled=True)
    tiles = call(order_body, shape, [SMEM, VMEM])(plan, tiles)
    tiles = lax.all_to_all(tiles, "section", 0, 0, tiled=True)
    own, copies, scale = call(
        norm_body,
        (
            jax.ShapeDtypeStruct((blocks, rows, width), bf16),
            jax.ShapeDtypeStruct((groups, blocks, rows, width), bf16),
            jax.ShapeDtypeStruct((1, width), jnp.float32),
        ),
        [VMEM, VMEM],
        n_out=3,
    )(tiles, gain_and_scale)

    all_rows = groups * blocks * rows
    normed = across_plane(copies.reshape(all_rows, width), sections, groups)
    spread = call(
        functools.partial(spread_body, part),
        jax.ShapeDtypeStruct((all_rows, sections * LANE), bf16),
        [VMEM],
    )(normed)
    partial_sum = call(
        functools.partial(mlp_body, part, units),
        jax.ShapeDtypeStruct((all_rows, width), bf16),
        [VMEM, ANY],
        flops=4 * all_rows * width * units,
        moved=10 * 1024 * 1024,
        scratch=[
            pltpu.VMEM((sections, 2 * kept, LANE), bf16),
            pltpu.SemaphoreType.DMA(()),
            pltpu.SemaphoreType.DMA(()),
        ],
        limit=50,
    )(spread, weights)
    terms = across_plane(partial_sum, sections, groups)
    return call(
        sum_body,
        jax.ShapeDtypeStruct((blocks, rows, width), bf16),
        [VMEM, VMEM, VMEM],
    )(terms.reshape(groups, blocks, rows, width), own, scale)


def solution(mesh):
    return jax.shard_map(
        functools.partial(local, mesh.shape["section"], mesh.shape["tensor"]),
        mesh=mesh,
        in_specs=(
            P("section", "tensor", None),
            P(),
            P(),
            P("section", "tensor"),
            P("tensor", "section"),
            P(),
        ),
        out_specs=P("section", "tensor", None),
        check_vma=False,
    )
```
